32 devices in a mesh: ctx: 8 (over z, x), fsdp: 4 (over y, core).
Axes of the slice: x: 2, y: 2, z: 4, core: 2. Of those that a mesh axis runs over, the one named last changes fastest.
Arguments:
- inputs: bfloat16 [1024, 8192], P('ctx', 'fsdp'), may hold values from -6 to 6
- upstream: bfloat16 [1024, 8192], P('ctx', 'fsdp'), may hold values from -6 to 6
- medium_filter: bfloat16 [512, 128], P('fsdp'), may hold values from -0.5 to 0.5
- short_filter: bfloat16 [512, 7], P('fsdp'), may hold values from -2 to 2
Outputs:
- input_gradient: bfloat16 [1024, 8192], P('ctx', 'fsdp')
- medium_gradient: float32 [512, 128], P('fsdp')
- short_gradient: float32 [512, 7], P('fsdp')
The draws below stay inside these ranges and needn't reach their ends.
All inputs are finite; a program needn't handle non-finite values.
Results may differ from the reference program's by a relative error of at most 0.005.
Values may be sent and summed in bfloat16 or wider, within the bound.
No kernel may reach another device: no remote copies, remote signals or barrier semaphores. Data moves between devices by JAX's collectives and lax.ppermute only.
A program may use at most 128 MiB of HBM per device.

```python
import math
import jax
import jax.numpy as jnp
from jax import lax

C = 8192
GROUP = 16
MED = 128
SHORT = 7
GROUPS = 512
LEN = 1024


def block_scale(rng, extent, shards, least, top_value):
    def one(dim, shards_of):
        draws = jax.random.uniform(jax.random.fold_in(jax.random.fold_in(rng, 6), dim), (shards_of,), jnp.float32, least / len(shards), top_value / len(shards))
        return jnp.repeat(jnp.exp(draws), extent[dim] // shards_of).reshape((-1,) + (1,) * (len(extent) - dim - 1))

    factor_of = one(*shards[0])
    for cut in shards[1:]:
        factor_of = factor_of * one(*cut)
    return factor_of


def centred(key, extent, scale, most, cuts=(), dtype=jnp.bfloat16):
    level = block_scale(key, extent, cuts, -0.22, 0.18) if cuts else 1.0
    drawn = jax.random.normal(key, extent, jnp.float32) * scale * level
    return jnp.minimum(jnp.maximum(drawn, -most), most).astype(dtype)


def setup_inputs(seed: int = 0) -> dict:
    seeds = jax.random.split(jax.random.key(seed), 5)
    return {
        "inputs": centred(seeds[0], (LEN, C), 1.0, 6.0, ((0, 8), (1, 4))),
        "upstream": centred(seeds[1], (LEN, C), 1.0, 6.0, ((0, 8), (1, 4))),
        "medium_filter": centred(seeds[2], (GROUPS, MED), MED ** -0.5, 0.5, ((0, 4),)),
        "short_filter": centred(seeds[3], (GROUPS, SHORT), SHORT ** -0.5, 2.0, ((0, 4),)),
    }


def reference(inputs, upstream, medium_filter, short_filter):
    block_width = math.gcd(C, 256)
    block_groups = block_width // GROUP
    block_count = C // block_width
    fft_points = 2 * LEN

    def one_block(index, carry):
        grads, medium_total, short_total = carry
        start = (index * block_width).astype(jnp.int32)
        row_start = (index * block_groups).astype(jnp.int32)
        values = lax.dynamic_slice_in_dim(inputs, start, block_width, 1).astype(jnp.float32)
        cot_values = lax.dynamic_slice_in_dim(upstream, start, block_width, 1).astype(jnp.float32)
        medium_rows = lax.dynamic_slice_in_dim(medium_filter, row_start, block_groups, 0).astype(jnp.float32)
        short_rows_in = lax.dynamic_slice_in_dim(short_filter, row_start, block_groups, 0).astype(jnp.float32)
        medium_channel = jnp.repeat(medium_rows, GROUP, axis=0)
        short_channel = jnp.repeat(short_rows_in, GROUP, axis=0)
        medium_freq = jnp.fft.rfft(medium_channel.T, n=fft_points, axis=0)
        token_freq = jnp.fft.rfft(values, n=fft_points, axis=0)
        conv = jnp.fft.irfft(token_freq * medium_freq, n=fft_points, axis=0)[:LEN]
        gate = jnp.zeros((LEN, block_width), jnp.float32)
        for tap_index in range(SHORT):
            shifted = jnp.pad(values, ((tap_index, 0), (0, 0)))[:LEN]
            gate = gate + short_channel[:, tap_index] * shifted
        gate_cot = (cot_values * conv).astype(jnp.bfloat16)
        conv_cot = (cot_values * gate).astype(jnp.bfloat16)
        gate_vals = gate_cot.astype(jnp.float32)
        conv_vals = conv_cot.astype(jnp.float32)
        cot_freq = jnp.fft.rfft(conv_vals, n=fft_points, axis=0)
        medium_back = jnp.fft.irfft(cot_freq * jnp.conj(medium_freq), n=fft_points, axis=0)[:LEN]
        short_back = jnp.zeros((LEN, block_width), jnp.float32)
        short_terms = []
        for tap_index in range(SHORT):
            ahead = jnp.pad(gate_vals, ((0, tap_index), (0, 0)))[tap_index:]
            short_back = short_back + short_channel[:, tap_index] * ahead
            shifted = jnp.pad(values, ((tap_index, 0), (0, 0)))[:LEN]
            short_terms.append(jnp.sum(gate_vals * shifted, axis=0))
        gradient = (medium_back + short_back).astype(jnp.bfloat16)
        cross = jnp.fft.irfft(cot_freq * jnp.conj(token_freq), n=fft_points, axis=0)[:MED]
        medium_sum = jnp.sum(cross.reshape(MED, block_groups, GROUP), axis=2).T
        short_sum = jnp.sum(jnp.stack(short_terms, axis=0).reshape(SHORT, block_groups, GROUP), axis=2).T
        grads = lax.dynamic_update_slice_in_dim(grads, gradient, start, 1)
        medium_total = lax.dynamic_update_slice_in_dim(medium_total, medium_sum, row_start, 0)
        short_total = lax.dynamic_update_slice_in_dim(short_total, short_sum, row_start, 0)
        return grads, medium_total, short_total

    initial = (jnp.zeros((LEN, C), jnp.bfloat16), jnp.zeros((GROUPS, MED), jnp.float32), jnp.zeros((GROUPS, SHORT), jnp.float32))
    grads, medium_total, short_total = lax.fori_loop(0, block_count, one_block, initial)
    factor = float(GROUP * LEN) ** -0.5
    return grads, medium_total * factor, short_total * factor
```

```python
import functools

import jax
import jax.numpy as jnp
from jax import lax
from jax.experimental import pallas as pl
from jax.experimental.pallas import tpu as pltpu
from jax.sharding import PartitionSpec as P

GROUP = 16
ROWS = 16
F32 = jnp.float32
BF16 = jnp.bfloat16


def iota(shape, dim):
    return lax.broadcasted_iota(jnp.int32, shape, dim)


def split3(values):
    high = values.astype(BF16)
    rest = values - high.astype(F32)
    middle = rest.astype(BF16)
    low = (rest - middle.astype(F32)).astype(BF16)
    return jnp.concatenate([high, middle, low], axis=0)


def exact_dot(values, table):
    rows = values.shape[0]
    out = jnp.dot(split3(values), table, preferred_element_type=F32)
    return out[:rows] + out[rows : 2 * rows] + out[2 * rows :]


def delayed(values, distance):
    return values if distance == 0 else pltpu.roll(values, distance, 0)


def toeplitz(base, table_ref):
    groups, lanes = base.shape
    for g in range(groups):
        row = jnp.broadcast_to(base[g : g + 1], (ROWS, lanes))
        table_ref[g * ROWS : (g + 1) * ROWS, :] = pltpu.roll(
            row, 0, 1, stride=1, stride_axis=0
        ).astype(BF16)


def own_group(product, lane_group):
    total = product[:ROWS]
    for g in range(1, product.shape[0] // ROWS):
        total = jnp.where(lane_group == g, product[g * ROWS : (g + 1) * ROWS], total)
    return total


def cot_kernel(taps, x_ref, u_ref, st_ref, *outs):
    cot_refs, wide_ref = outs[:-1], outs[-1]
    rows, cols = x_ref.shape
    groups = st_ref.shape[1]
    first = pl.program_id(0) * (cols // GROUP)
    spread = iota((groups, cols), 0) == first + iota((groups, cols), 1) // GROUP
    wide = jnp.dot(st_ref[...], spread.astype(BF16), preferred_element_type=F32)
    wide_ref[...] = wide
    x = x_ref[...].astype(F32)
    gate = wide[0:1] * x
    for j in range(1, taps):
        gate = gate + wide[j : j + 1] * delayed(x, j)
    cot = (u_ref[...].astype(F32) * gate).astype(BF16)[ROWS:]
    if len(cot_refs) == 1:
        cot_refs[0][...] = cot
    else:
        steps = pl.num_programs(0) // len(cot_refs)
        for i, ref in enumerate(cot_refs):

            @pl.when(pl.program_id(0) // steps == i)
            def _():
                ref[...] = cot


def sum_kernel(taps, factor, first_step, m_ref, prev_ref, x_ref, u_ref, cot_ref, wide_ref,
               *rest):
    sums_in, rest = (rest[0], rest[1:]) if len(rest) == 6 else (None, rest)
    gate_cot_ref, edge_ref, sums_ref, x_ext, table = rest
    rows, cols = x_ref.shape
    halo = prev_ref.shape[0]
    med = m_ref.shape[1]
    groups = m_ref.shape[0]
    window = med + ROWS
    lanes = table.shape[1]
    step = pl.program_id(0)
    total_groups = sums_ref.shape[0] - 8

    if sums_in is None:

        @pl.when(step == 0)
        def _():
            sums_ref[...] = jnp.zeros_like(sums_ref)

    else:

        @pl.when(step == 0)
        def _():
            sums_ref[...] = sums_in[...]

    x_ext[:halo, :] = prev_ref[...]
    x_ext[halo:, :] = x_ref[...]
    flip = iota((med, lanes), 0) == med - iota((med, lanes), 1)
    toeplitz(jnp.dot(m_ref[...], flip.astype(BF16), preferred_element_type=F32), table)
    lane_group = iota((ROWS, cols), 1) // GROUP

    x_near = x_ext[halo - ROWS :, :].astype(F32)
    wide = wide_ref[...]
    head = x_near[: 2 * ROWS]
    gate = wide[0:1] * head
    for j in range(1, taps):
        gate = gate + wide[j : j + 1] * delayed(head, j)
    head_cot = (u_ref[:ROWS, :].astype(F32) * gate[ROWS:]).astype(BF16)
    edge_ref[:ROWS, :] = head_cot

    upturn = iota((rows, rows), 0) ^ (ROWS - 1) == iota((rows, rows), 1)
    cots = jnp.concatenate([head_cot, cot_ref[...]], 0)
    cots = jnp.dot(upturn.astype(BF16), cots, preferred_element_type=F32).astype(BF16)

    pairs = jnp.zeros((groups * ROWS, window), F32)
    for a in range(rows // ROWS):
        here = slice(a * ROWS, (a + 1) * ROWS)
        part = x_ext[a * ROWS : a * ROWS + window, :]
        conv = own_group(
            jnp.dot(table[:, :window], part, preferred_element_type=F32), lane_group
        )
        gate_cot_ref[here, :] = (u_ref[here, :].astype(F32) * conv).astype(BF16)
        cot = cots[here]
        alone = jnp.concatenate(
            [jnp.where(lane_group == g, cot, jnp.zeros_like(cot)) for g in range(groups)], 0
        )
        pairs = pairs + lax.dot_general(
            alone, part, (((1,), (1,)), ((), ())), preferred_element_type=F32
        )
    edge_ref[ROWS:, :] = gate_cot_ref[:ROWS, :]

    pairs = jnp.concatenate([pairs, jnp.zeros((groups * ROWS, lanes - window), F32)], 1)
    diagonals = []
    for g in range(groups):
        block = pltpu.roll(
            pairs[g * ROWS : (g + 1) * ROWS], 0, 1, stride=1, stride_axis=0
        )
        diagonals.append(jnp.sum(block, 0, keepdims=True))
    flip_back = iota((lanes, med), 0) == med + ROWS - 1 - iota((lanes, med), 1)
    medium = exact_dot(jnp.concatenate(diagonals, 0), flip_back.astype(BF16))
    at = pl.multiple_of((first_step + step) * groups, groups)
    sums_ref[pl.ds(at, groups), :] = medium * factor

    gate_cot = gate_cot_ref[...].astype(F32)
    short = [
        jnp.sum(gate_cot * delayed(x_near, j)[ROWS:], 0, keepdims=True) for j in range(taps)
    ]
    short.append(jnp.zeros((8 - taps, cols), F32))
    gather = (
        iota((cols, med), 1) == (first_step + step) * groups + iota((cols, med), 0) // GROUP
    )
    sums_ref[total_groups:, :] += (
        exact_dot(jnp.concatenate(short, 0), gather.astype(BF16)) * factor
    )


def back_kernel(ms_ref, cot_ref, gate_cot_ref, edge_ref, next_ref, next_edge_ref, out_ref,
                c_ext, g_ext, table):
    rows, cols = gate_cot_ref.shape
    med = next_ref.shape[0] + ROWS
    window = med + ROWS
    toeplitz(ms_ref[...].astype(F32), table)
    lane_group = iota((ROWS, cols), 1) // GROUP
    c_ext[:ROWS, :] = edge_ref[:ROWS, :]
    c_ext[ROWS:rows, :] = cot_ref[...]
    c_ext[rows : rows + ROWS, :] = next_edge_ref[:ROWS, :]
    c_ext[rows + ROWS :, :] = next_ref[...]
    g_ext[:rows, :] = gate_cot_ref[...]
    g_ext[rows:, :] = next_edge_ref[ROWS:, :]
    for a in range(rows // ROWS):
        part = jnp.concatenate(
            [
                c_ext[a * ROWS : a * ROWS + window, :],
                g_ext[a * ROWS : (a + 2) * ROWS, :],
            ],
            0,
        )
        product = jnp.dot(
            table[:, : window + 2 * ROWS], part, preferred_element_type=F32
        )
        out_ref[a * ROWS : (a + 1) * ROWS, :] = own_group(product, lane_group).astype(BF16)


def permuted(block, pairs):
    return lax.ppermute(block, "ctx", pairs)


def local(inputs, upstream, medium_filter, short_filter):
    rows, width = inputs.shape
    groups, med = medium_filter.shape
    taps = short_filter.shape[1]
    devices = lax.axis_size("ctx")
    assert rows % ROWS == 0 and rows >= med and med % 128 == 0 and groups <= med
    assert taps <= 8
    cols = 256 if width % 256 == 0 else width
    chunks = 2 if width % (2 * cols) == 0 else 1
    steps = width // cols // chunks
    part = steps * cols
    tile = cols // GROUP
    lanes = med + 128
    factor = float(GROUP * rows * devices) ** -0.5
    forward = [(i, i + 1) for i in range(devices - 1)]
    backward = [(i + 1, i) for i in range(devices - 1)]
    limit = 48 << 20

    def params():
        return pltpu.CompilerParams(vmem_limit_bytes=limit)

    tail = inputs[rows - med :]
    previous = [permuted(tail[:, i * part : (i + 1) * part], forward) for i in range(chunks)]

    short_rows = jnp.pad(short_filter.T, ((0, 8 - taps), (0, 0)))
    whole = lambda i: (0, 0)
    along = lambda i: (0, i)

    def held(k):
        return lambda i: (0, jnp.clip(i - k * steps, 0, steps - 1))

    *cots, wide = pl.pallas_call(
        functools.partial(cot_kernel, taps),
        grid=(chunks * steps,),
        in_specs=[
            pl.BlockSpec((rows, cols), along),
            pl.BlockSpec((rows, cols), along),
            pl.BlockSpec((8, groups), whole),
        ],
        out_specs=[pl.BlockSpec((rows - ROWS, cols), held(k)) for k in range(chunks)]
        + [pl.BlockSpec((8, cols), along)],
        out_shape=[jax.ShapeDtypeStruct((rows - ROWS, part), BF16)] * chunks
        + [jax.ShapeDtypeStruct((8, width), F32)],
        compiler_params=params(),
        name="conv_cot",
    )(inputs, upstream, short_rows)

    following = [permuted(c[: med - ROWS], backward) for c in cots]

    gate_cots, edges, sums = [], [], None
    for k in range(chunks):
        base = k * steps
        shift = lambda i, base=base: (0, base + i)
        in_specs = [
            pl.BlockSpec((tile, med), lambda i, base=base: (base + i, 0)),
            pl.BlockSpec((med, cols), along),
            pl.BlockSpec((rows, cols), shift),
            pl.BlockSpec((rows, cols), shift),
            pl.BlockSpec((rows - ROWS, cols), along),
            pl.BlockSpec((8, cols), shift),
        ]
        operands = [medium_filter, previous[k], inputs, upstream, cots[k], wide]
        if k:
            in_specs.append(pl.BlockSpec((groups + 8, med), whole))
            operands.append(sums)
        gate_cot, edge, sums = pl.pallas_call(
            functools.partial(sum_kernel, taps, factor, base),
            grid=(steps,),
            in_specs=in_specs,
            out_specs=[
                pl.BlockSpec((rows, cols), along),
                pl.BlockSpec((2 * ROWS, cols), along),
                pl.BlockSpec((groups + 8, med), whole),
            ],
            out_shape=[
                jax.ShapeDtypeStruct((rows, part), BF16),
                jax.ShapeDtypeStruct((2 * ROWS, part), BF16),
                jax.ShapeDtypeStruct((groups + 8, med), F32),
            ],
            scratch_shapes=[
                pltpu.VMEM((med + rows, cols), BF16),
                pltpu.VMEM((tile * ROWS, lanes), BF16),
            ],
            compiler_params=params(),
            name="filter_sums",
        )(*operands)
        gate_cots.append(gate_cot)
        edges.append(edge)

    next_edges = [permuted(e, backward) for e in edges]

    if devices & (devices - 1):
        sums = lax.psum(sums, "ctx")
    else:
        reach = 1
        while reach < devices:
            sums = sums + permuted(sums, [(i, i ^ reach) for i in range(devices)])
            reach *= 2

    both = jnp.pad(medium_filter, ((0, 0), (0, lanes - med))) + jnp.pad(
        short_filter, ((0, 0), (med + ROWS, lanes - med - ROWS - taps))
    )
    pieces = []
    for k in range(chunks):
        base = k * steps
        pieces.append(
            pl.pallas_call(
                back_kernel,
                grid=(steps,),
                in_specs=[
                    pl.BlockSpec((tile, lanes), lambda i, base=base: (base + i, 0)),
                    pl.BlockSpec((rows - ROWS, cols), along),
                    pl.BlockSpec((rows, cols), along),
                    pl.BlockSpec((2 * ROWS, cols), along),
                    pl.BlockSpec((med - ROWS, cols), along),
                    pl.BlockSpec((2 * ROWS, cols), along),
                ],
                out_specs=pl.BlockSpec((rows, cols), along),
                out_shape=jax.ShapeDtypeStruct((rows, part), BF16),
                scratch_shapes=[
                    pltpu.VMEM((rows + med, cols), BF16),
                    pltpu.VMEM((rows + ROWS, cols), BF16),
                    pltpu.VMEM((tile * ROWS, lanes), BF16),
                ],
                compiler_params=params(),
                name="input_grad",
            )(both, cots[k], gate_cots[k], edges[k], following[k], next_edges[k])
        )
    input_gradient = jnp.concatenate(pieces, axis=1)
    return input_gradient, sums[:groups], sums[groups : groups + taps, :groups].T


def solution(mesh):
    return jax.shard_map(
        local,
        mesh=mesh,
        in_specs=(P("ctx", "fsdp"), P("ctx", "fsdp"), P("fsdp", None), P("fsdp", None)),
        out_specs=(P("ctx", "fsdp"), P("fsdp", None), P("fsdp", None)),
        check_vma=False,
    )
```

```python
import functools

import jax
import jax.numpy as jnp
from jax import lax
from jax.experimental import pallas as pl
from jax.experimental.pallas import tpu as pltpu
from jax.sharding import PartitionSpec as P

GROUP = 16
ROWS = 16
LANES = 128
F32 = jnp.float32
BF16 = jnp.bfloat16


def iota(shape, dim):
    return lax.broadcasted_iota(jnp.int32, shape, dim)


def split3(values):
    high = values.astype(BF16)
    rest = values - high.astype(F32)
    middle = rest.astype(BF16)
    low = (rest - middle.astype(F32)).astype(BF16)
    return jnp.concatenate([high, middle, low], axis=0)


def exact_dot(values, table):
    rows = values.shape[0]
    out = jnp.dot(split3(values), table, preferred_element_type=F32)
    return out[:rows] + out[rows : 2 * rows] + out[2 * rows :]


def delayed(values, distance):
    return values if distance == 0 else pltpu.roll(values, distance, 0)


def toeplitz(base):
    lanes = base.shape[1]
    blocks = [
        pltpu.roll(
            jnp.broadcast_to(base[g : g + 1], (ROWS, lanes)), 0, 1, stride=1, stride_axis=0
        )
        for g in range(base.shape[0])
    ]
    return jnp.concatenate(blocks, 0).astype(BF16)


def own_group(product, lane_group):
    total = product[:ROWS]
    for g in range(1, product.shape[0] // ROWS):
        total = jnp.where(lane_group == g, product[g * ROWS : (g + 1) * ROWS], total)
    return total


def stacked(first, second, start, stop):
    extent = first.shape[0]
    if stop <= extent:
        return first[start:stop]
    if start >= extent:
        return second[start - extent : stop - extent]
    return jnp.concatenate([first[start:], second[: stop - extent]], 0)


def sum_kernel(taps, factor, first_step, m_ref, st_ref, prev_ref, x_ref, u_ref, *rest):
    sums_in, rest = (rest[0], rest[1:]) if len(rest) == 4 else (None, rest)
    gate_cot_ref, cot_ref, sums_ref = rest
    rows, cols = x_ref.shape
    groups, med = m_ref.shape
    window = med + ROWS
    lanes = med + 128
    tile = LANES // GROUP
    step = pl.program_id(0)
    here = (first_step + step) * groups
    total_groups = sums_ref.shape[0] - 8

    @pl.when(step == 0)
    def _():
        sums_ref[...] = jnp.zeros_like(sums_ref) if sums_in is None else sums_in[...]

    flip = iota((med, lanes), 0) == med - iota((med, lanes), 1)
    base = jnp.dot(m_ref[...], flip.astype(BF16), preferred_element_type=F32)
    spread = iota((st_ref.shape[1], cols), 0) == here + iota((st_ref.shape[1], cols), 1) // GROUP
    wide = jnp.dot(st_ref[...], spread.astype(BF16), preferred_element_type=F32)
    upturn = (iota((rows, rows), 0) ^ (ROWS - 1) == iota((rows, rows), 1)).astype(BF16)
    lane_group = iota((ROWS, 2 * LANES), 1) % LANES // GROUP

    diagonals, short = [], []
    for block in range(cols // LANES):
        at = slice(block * LANES, (block + 1) * LANES)
        prev, x = prev_ref[:, at], x_ref[:, at]
        u = u_ref[:, at].astype(F32)
        near = jnp.concatenate([prev[med - ROWS :], x], 0).astype(F32)
        late = [delayed(near, j)[ROWS:] for j in range(taps)]
        gate = wide[0:1, at] * late[0]
        for j in range(1, taps):
            gate = gate + wide[j : j + 1, at] * late[j]
        cot = (u * gate).astype(BF16)
        cot_ref[ROWS:, at] = cot
        upturned = jnp.dot(upturn, cot, preferred_element_type=F32).astype(BF16)
        table = toeplitz(base[block * tile : (block + 1) * tile])[:, :window]

        pairs = jnp.zeros((tile * ROWS, window), F32)
        gate_cots = []
        for a in range(0, rows // ROWS, 2):
            lo, mid, hi = (ROWS * k for k in (a, a + 1, a + 2))
            part = jnp.concatenate(
                [stacked(prev, x, k, k + window) for k in (lo, mid)], 1
            )
            conv = own_group(jnp.dot(table, part, preferred_element_type=F32), lane_group)
            for k in range(2):
                gate_cots.append(
                    (u[lo + k * ROWS : mid + k * ROWS] * conv[:, k * LANES : (k + 1) * LANES])
                    .astype(BF16)
                )
            both = jnp.concatenate([upturned[lo:mid], upturned[mid:hi]], 1)
            alone = jnp.concatenate(
                [jnp.where(lane_group == g, both, jnp.zeros_like(both)) for g in range(tile)], 0
            )
            pairs = pairs + lax.dot_general(
                alone, part, (((1,), (1,)), ((), ())), preferred_element_type=F32
            )
        gate_cot = jnp.concatenate(gate_cots, 0)
        gate_cot_ref[:, at] = gate_cot
        cot_ref[:ROWS, at] = gate_cot[:ROWS]

        pairs = jnp.concatenate([pairs, jnp.zeros((tile * ROWS, lanes - window), F32)], 1)
        for g in range(tile):
            diagonals.append(
                jnp.sum(
                    pltpu.roll(
                        pairs[g * ROWS : (g + 1) * ROWS], 0, 1, stride=1, stride_axis=0
                    ),
                    0,
                    keepdims=True,
                )
            )
        gate_cot = gate_cot.astype(F32)
        sums = [jnp.sum(gate_cot * late[j], 0, keepdims=True) for j in range(taps)]
        short.append(jnp.concatenate(sums + [jnp.zeros((8 - taps, LANES), F32)], 0))

    flip_back = iota((lanes, med), 0) == med + ROWS - 1 - iota((lanes, med), 1)
    medium = exact_dot(jnp.concatenate(diagonals, 0), flip_back.astype(BF16))
    sums_ref[pl.ds(pl.multiple_of(here, groups), groups), :] = medium * factor
    gather = iota((cols, med), 1) == here + iota((cols, med), 0) // GROUP
    sums_ref[total_groups:, :] += (
        exact_dot(jnp.concatenate(short, 1), gather.astype(BF16)) * factor
    )


def back_kernel(ms_ref, gate_cot_ref, cot_ref, next_ref, *rest):
    out_ref = rest[-1]
    rows, cols = gate_cot_ref.shape
    window = next_ref.shape[0]
    tile = LANES // GROUP
    base = ms_ref[...].astype(F32)
    lane_group = iota((ROWS, 2 * LANES), 1) % LANES // GROUP
    for block in range(cols // LANES):
        at = slice(block * LANES, (block + 1) * LANES)
        table = toeplitz(base[block * tile : (block + 1) * tile])[:, : window + 2 * ROWS]
        cot, after = cot_ref[ROWS:, at], next_ref[ROWS:, at]
        gate_cot, gate_after = gate_cot_ref[:, at], next_ref[:ROWS, at]
        for a in range(0, rows // ROWS, 2):
            sides = []
            for k in (a * ROWS, (a + 1) * ROWS):
                sides.append(
                    jnp.concatenate(
                        [
                            stacked(cot, after, k, k + window),
                            stacked(gate_cot, gate_after, k, k + 2 * ROWS),
                        ],
                        0,
                    )
                )
            product = jnp.dot(
                table, jnp.concatenate(sides, 1), preferred_element_type=F32
            )
            out = own_group(product, lane_group).astype(BF16)
            out_ref[a * ROWS : (a + 1) * ROWS, at] = out[:, :LANES]
            out_ref[(a + 1) * ROWS : (a + 2) * ROWS, at] = out[:, LANES:]


def permuted(block, pairs):
    return lax.ppermute(block, "ctx", pairs)


def local(inputs, upstream, medium_filter, short_filter):
    rows, width = inputs.shape
    groups, med = medium_filter.shape
    taps = short_filter.shape[1]
    devices = lax.axis_size("ctx")
    assert rows % (2 * ROWS) == 0 and rows >= med and med % 128 == 0 and groups <= med
    assert taps <= 8 and width % LANES == 0
    chunks = 2 if width % (4 * LANES) == 0 else 1
    part = width // chunks
    cols = max(c for c in (4 * LANES, 2 * LANES, LANES) if part % c == 0)
    steps = part // cols
    tile = cols // GROUP
    lanes = med + 128
    factor = float(GROUP * rows * devices) ** -0.5
    forward = [(i, i + 1) for i in range(devices - 1)]
    backward = [(i + 1, i) for i in range(devices - 1)]

    def params():
        return pltpu.CompilerParams(vmem_limit_bytes=48 << 20)

    whole = lambda i: (0, 0)
    along = lambda i: (0, i)

    tail = inputs[rows - med :]
    previous = [permuted(tail[:, i * part : (i + 1) * part], forward) for i in range(chunks)]
    short_rows = jnp.pad(short_filter.T, ((0, 8 - taps), (0, 0)))

    gate_cots, cots, following, sums = [], [], [], None
    for k in range(chunks):
        base = k * steps
        shift = lambda i, base=base: (0, base + i)
        in_specs = [
            pl.BlockSpec((tile, med), lambda i, base=base: (base + i, 0)),
            pl.BlockSpec((8, groups), whole),
            pl.BlockSpec((med, cols), along),
            pl.BlockSpec((rows, cols), shift),
            pl.BlockSpec((rows, cols), shift),
        ]
        operands = [medium_filter, short_rows, previous[k], inputs, upstream]
        if k:
            in_specs.append(pl.BlockSpec((groups + 8, med), whole))
            operands.append(sums)
        gate_cot, cot, sums = pl.pallas_call(
            functools.partial(sum_kernel, taps, factor, base),
            grid=(steps,),
            in_specs=in_specs,
            out_specs=[
                pl.BlockSpec((rows, cols), along),
                pl.BlockSpec((rows + ROWS, cols), along),
                pl.BlockSpec((groups + 8, med), whole),
            ],
            out_shape=[
                jax.ShapeDtypeStruct((rows, part), BF16),
                jax.ShapeDtypeStruct((rows + ROWS, part), BF16),
                jax.ShapeDtypeStruct((groups + 8, med), F32),
            ],
            compiler_params=params(),
            name="filter_sums",
        )(*operands)
        gate_cots.append(gate_cot)
        cots.append(cot)
        following.append(permuted(cot[: med + ROWS], backward))

    if devices & (devices - 1):
        sums = lax.psum(sums, "ctx")
    else:
        reach = 1
        while reach < devices:
            sums = sums + permuted(sums, [(i, i ^ reach) for i in range(devices)])
            reach *= 2

    both = jnp.pad(medium_filter, ((0, 0), (0, lanes - med))) + jnp.pad(
        short_filter, ((0, 0), (med + ROWS, lanes - med - ROWS - taps))
    )
    gradient = None
    for k in range(chunks):
        base = k * steps
        in_specs = [
            pl.BlockSpec((tile, lanes), lambda i, base=base: (base + i, 0)),
            pl.BlockSpec((rows, cols), along),
            pl.BlockSpec((rows + ROWS, cols), along),
            pl.BlockSpec((med + ROWS, cols), along),
        ]
        operands = [both, gate_cots[k], cots[k], following[k]]
        if k:
            in_specs.append(pl.BlockSpec(memory_space=pl.ANY))
            operands.append(gradient)
        gradient = pl.pallas_call(
            back_kernel,
            grid=(steps,),
            in_specs=in_specs,
            out_specs=pl.BlockSpec((rows, cols), lambda i, base=base: (0, base + i)),
            out_shape=jax.ShapeDtypeStruct((rows, width), BF16),
            input_output_aliases={4: 0} if k else {},
            compiler_params=params(),
            name="input_grad",
        )(*operands)
    return gradient, sums[:groups], sums[groups : groups + taps, :groups].T


def solution(mesh):
    return jax.shard_map(
        local,
        mesh=mesh,
        in_specs=(P("ctx", "fsdp"), P("ctx", "fsdp"), P("fsdp", None), P("fsdp", None)),
        out_specs=(P("ctx", "fsdp"), P("fsdp", None), P("fsdp", None)),
        check_vma=False,
    )
```

```python
import functools

import jax
import jax.numpy as jnp
from jax import lax
from jax.experimental import pallas as pl
from jax.experimental.pallas import tpu as pltpu
from jax.sharding import PartitionSpec as P

GROUP = 16
ROWS = 16
LANES = 128
F32 = jnp.float32
BF16 = jnp.bfloat16
SMALL = pl.CostEstimate(flops=1, bytes_accessed=1, transcendentals=0)


def iota(shape, dim):
    return lax.broadcasted_iota(jnp.int32, shape, dim)


def split3(values):
    high = values.astype(BF16)
    rest = values - high.astype(F32)
    middle = rest.astype(BF16)
    low = (rest - middle.astype(F32)).astype(BF16)
    return jnp.concatenate([high, middle, low], axis=0)


def exact_dot(values, table):
    rows = values.shape[0]
    out = jnp.dot(split3(values), table, preferred_element_type=F32)
    return out[:rows] + out[rows : 2 * rows] + out[2 * rows :]


def delayed(values, distance):
    return values if distance == 0 else pltpu.roll(values, distance, 0)


def toeplitz(base):
    lanes = base.shape[1]
    blocks = [
        pltpu.roll(
            jnp.broadcast_to(base[g : g + 1], (ROWS, lanes)), 0, 1, stride=1, stride_axis=0
        )
        for g in range(base.shape[0])
    ]
    return jnp.concatenate(blocks, 0).astype(BF16)


def own_group(product, lane_group):
    total = product[:ROWS]
    for g in range(1, product.shape[0] // ROWS):
        total = jnp.where(lane_group == g, product[g * ROWS : (g + 1) * ROWS], total)
    return total


def stacked(first, second, start, stop):
    extent = first.shape[0]
    if stop <= extent:
        return first[start:stop]
    if start >= extent:
        return second[start - extent : stop - extent]
    return jnp.concatenate([first[start:], second[: stop - extent]], 0)


def masked(cots, lane_group):
    return jnp.concatenate(
        [
            jnp.where(lane_group == g, cots, jnp.zeros_like(cots))
            for g in range(LANES // GROUP)
        ],
        0,
    )


def contracted(alone, part):
    return lax.dot_general(
        alone, part, (((1,), (1,)), ((), ())), preferred_element_type=F32
    )


def diagonal_sums(pairs, lanes):
    if pairs.shape[1] < lanes:
        pad = jnp.zeros((pairs.shape[0], lanes - pairs.shape[1]), F32)
        pairs = jnp.concatenate([pairs, pad], 1)
    return [
        jnp.sum(
            pltpu.roll(pairs[g * ROWS : (g + 1) * ROWS], 0, 1, stride=1, stride_axis=0),
            0,
            keepdims=True,
        )
        for g in range(LANES // GROUP)
    ]


def medium_sums(diagonals, med, lanes):
    flip_back = iota((lanes, med), 0) == med + ROWS - 1 - iota((lanes, med), 1)
    return exact_dot(jnp.concatenate(diagonals, 0), flip_back.astype(BF16))


def turning(extent):
    return (iota((extent, extent), 0) ^ (ROWS - 1) == iota((extent, extent), 1)).astype(BF16)


def gated(wide, near, taps):
    gate = wide[0:1] * near[ROWS:]
    for j in range(1, taps):
        gate = gate + wide[j : j + 1] * delayed(near, j)[ROWS:]
    return gate


def lane_groups():
    return iota((ROWS, 2 * LANES), 1) % LANES // GROUP


def own_kernel(taps, pieces, m_ref, st_ref, x_ref, u_ref, *outs):
    *send_refs, turned_ref, conv_ref, medium_ref, table_ref, wide_ref, made = outs
    rows, cols = x_ref.shape
    groups, med = m_ref.shape
    window = med + ROWS
    lanes = med + 128
    tile = LANES // GROUP
    first = pl.program_id(0) * groups

    flip = iota((med, lanes), 0) == med - iota((med, lanes), 1)
    base = jnp.dot(m_ref[...], flip.astype(BF16), preferred_element_type=F32)
    spread = iota((st_ref.shape[1], cols), 0) == first + iota((st_ref.shape[1], cols), 1) // GROUP
    wide_ref[...] = jnp.dot(st_ref[...], spread.astype(BF16), preferred_element_type=F32)
    made[rows - ROWS : rows, :] = x_ref[:ROWS, :]
    made[rows:, :] = u_ref[:ROWS, :]
    upturn = turning(rows)
    lane_group = lane_groups()

    diagonals = []
    for block in range(cols // LANES):
        at = slice(block * LANES, (block + 1) * LANES)
        x = x_ref[:, at]
        near = jnp.concatenate([jnp.zeros((ROWS, LANES), F32), x.astype(F32)], 0)
        cot = (u_ref[:, at].astype(F32) * gated(wide_ref[:, at], near, taps)).astype(BF16)
        made[: rows - ROWS, at] = cot[ROWS:]
        turned = jnp.dot(upturn, cot, preferred_element_type=F32).astype(BF16)
        turned_ref[:, at] = turned
        table = toeplitz(base[block * tile : (block + 1) * tile])
        table_ref[block * LANES : (block + 1) * LANES, :] = table

        pairs = jnp.zeros((LANES, window), F32)
        for a in range(0, rows // ROWS, 2):
            lo, mid, hi = (ROWS * k for k in (a, a + 1, a + 2))
            empty = jnp.zeros((med - lo, LANES), BF16)
            part = jnp.concatenate(
                [
                    jnp.concatenate([empty, x[:mid]], 0),
                    jnp.concatenate([empty, x[ROWS:hi]], 0),
                ],
                1,
            )
            conv = own_group(
                jnp.dot(table[:, :window], part, preferred_element_type=F32), lane_group
            )
            conv_ref[lo:mid, at] = conv[:, :LANES]
            conv_ref[mid:hi, at] = conv[:, LANES:]
            if a:
                both = jnp.concatenate([turned[lo:mid], turned[mid:hi]], 1)
                pairs = pairs + contracted(masked(both, lane_group), part)
        diagonals += diagonal_sums(pairs, lanes)
    medium_ref[...] = medium_sums(diagonals, med, lanes)

    step = pl.program_id(0)
    for send_ref, (start, count) in zip(send_refs, pieces):

        @pl.when(jnp.logical_and(step >= start, step < start + count))
        def _(send_ref=send_ref):
            send_ref[...] = made[...]


def halo_kernel(taps, factor, table_ref, wide_ref, prev_ref, x_ref, u_ref, turned_ref,
                conv_ref, medium_ref, *rest):
    gate_cot_ref, sums_ref = rest[:2] if len(rest) == 2 else rest[1:3]
    rows, cols = x_ref.shape
    med = prev_ref.shape[0]
    groups = medium_ref.shape[0]
    window = med + ROWS
    lanes = med + 128
    step = pl.program_id(0)
    first = step * groups
    total_groups = sums_ref.shape[0] - 8

    @pl.when(step == 0)
    def _():
        sums_ref[total_groups:, :] = jnp.zeros((8, med), F32)

    upturn = turning(ROWS)
    lane_group = lane_groups()
    diagonals, short = [], []
    for block in range(cols // LANES):
        at = slice(block * LANES, (block + 1) * LANES)
        prev, x, u = prev_ref[:, at], x_ref[:, at], u_ref[:, at]
        near = jnp.concatenate([prev[med - ROWS :], x], 0).astype(F32)
        table = table_ref[block * LANES : (block + 1) * LANES, :]
        head = gated(wide_ref[:, at], near[: 2 * ROWS], taps) * u[:ROWS].astype(F32)
        head = head.astype(BF16)
        gate_cot_ref[:ROWS, at] = head
        head = jnp.dot(upturn, head, preferred_element_type=F32).astype(BF16)

        pairs = None
        gate_cots = []
        for a in range(0, rows // ROWS, 2):
            lo, mid, hi = (ROWS * k for k in (a, a + 1, a + 2))
            if a and med <= lo:
                conv = jnp.zeros((ROWS, 2 * LANES), F32)
            else:
                part = jnp.concatenate(
                    [stacked(prev, x, lo, med), stacked(prev, x, mid, med + ROWS)], 1
                )
                conv = own_group(
                    jnp.dot(table[:, : med - lo], part, preferred_element_type=F32),
                    lane_group,
                )
                if a == 0:
                    part = jnp.concatenate([part, jnp.concatenate([x[:ROWS], x[ROWS:hi]], 1)], 0)
                    both = jnp.concatenate([head, turned_ref[mid:hi, at]], 1)
                else:
                    both = jnp.concatenate([turned_ref[lo:mid, at], turned_ref[mid:hi, at]], 1)
                more = contracted(masked(both, lane_group), part)
                if more.shape[1] < window:
                    more = jnp.concatenate(
                        [more, jnp.zeros((LANES, window - more.shape[1]), F32)], 1
                    )
                pairs = more if pairs is None else pairs + more
            for k in range(2):
                here = slice(lo + k * ROWS, mid + k * ROWS)
                whole = conv_ref[here, at] + conv[:, k * LANES : (k + 1) * LANES]
                gate_cots.append((u[here].astype(F32) * whole).astype(BF16))
        gate_cot = jnp.concatenate(gate_cots, 0)
        gate_cot_ref[ROWS:, at] = gate_cot
        diagonals += diagonal_sums(pairs, lanes)
        gate_cot = gate_cot.astype(F32)
        sums = [
            jnp.sum(gate_cot * delayed(near, j)[ROWS:], 0, keepdims=True) for j in range(taps)
        ]
        short.append(jnp.concatenate(sums + [jnp.zeros((8 - taps, LANES), F32)], 0))

    medium = medium_ref[...] + medium_sums(diagonals, med, lanes)
    sums_ref[pl.ds(pl.multiple_of(first, groups), groups), :] = medium * factor
    gather = iota((cols, med), 1) == first + iota((cols, med), 0) // GROUP
    sums_ref[total_groups:, :] += (
        exact_dot(jnp.concatenate(short, 1), gather.astype(BF16)) * factor
    )


def back_kernel(taps, ms_ref, table_ref, wide_ref, x_ref, gate_cot_ref, cot_ref, next_ref, *rest):
    out_ref = rest[-1]
    rows, cols = x_ref.shape
    window = table_ref.shape[1] - 128 + ROWS
    tile = LANES // GROUP
    base = ms_ref[...].astype(F32)
    lane_group = lane_groups()
    for block in range(cols // LANES):
        at = slice(block * LANES, (block + 1) * LANES)
        forward = table_ref[block * LANES : (block + 1) * LANES, :window]
        table = toeplitz(base[block * tile : (block + 1) * tile])[:, : window + 2 * ROWS]
        x, x_next = x_ref[:, at], next_ref[rows - ROWS : rows, at]
        u_next = next_ref[rows:, at].astype(F32)
        near = jnp.concatenate([x[rows - ROWS :], x_next], 0).astype(F32)
        head = (u_next * gated(wide_ref[:, at], near, taps)).astype(BF16)
        part = jnp.concatenate([x[rows + ROWS - window :], x_next], 0)
        conv = jnp.dot(forward, part, preferred_element_type=F32)
        gate_after = (u_next * own_group(conv, lane_group[:, :LANES])).astype(BF16)
        cot = jnp.concatenate([gate_cot_ref[:ROWS, at], cot_ref[: rows - ROWS, at]], 0)
        after = jnp.concatenate([head, next_ref[: rows - ROWS, at]], 0)
        gate_cot = gate_cot_ref[ROWS:, at]
        for a in range(0, rows // ROWS, 2):
            sides = [
                jnp.concatenate(
                    [
                        stacked(cot, after, k, k + window),
                        stacked(gate_cot, gate_after, k, k + 2 * ROWS),
                    ],
                    0,
                )
                for k in (a * ROWS, (a + 1) * ROWS)
            ]
            product = jnp.dot(
                table, jnp.concatenate(sides, 1), preferred_element_type=F32
            )
            out = own_group(product, lane_group).astype(BF16)
            out_ref[a * ROWS : (a + 1) * ROWS, at] = out[:, :LANES]
            out_ref[(a + 1) * ROWS : (a + 2) * ROWS, at] = out[:, LANES:]


def add_kernel(own_ref, other_ref, held_ref, out_ref, held_out_ref):
    out_ref[...] = own_ref[...] + other_ref[...]


def add_after(own, other, held):
    return pl.pallas_call(
        add_kernel,
        in_specs=[pl.BlockSpec(own.shape, lambda: (0, 0))] * 2
        + [pl.BlockSpec(memory_space=pl.ANY)],
        out_specs=[
            pl.BlockSpec(own.shape, lambda: (0, 0)),
            pl.BlockSpec(memory_space=pl.ANY),
        ],
        out_shape=[
            jax.ShapeDtypeStruct(own.shape, own.dtype),
            jax.ShapeDtypeStruct(held.shape, held.dtype),
        ],
        input_output_aliases={2: 1},
        compiler_params=pltpu.CompilerParams(vmem_limit_bytes=16 << 20),
        cost_estimate=SMALL,
        name="add_sums",
    )(own, other, held)


def finish_kernel(groups, taps, own_ref, other_ref, held_ref, medium_ref, short_ref, held_out_ref):
    total = own_ref[...] + other_ref[...]
    medium_ref[...] = total[:groups]
    short_ref[...] = total[groups : groups + taps, :groups]


def finish(own, other, held, groups, taps):
    lanes = own.shape[1]
    return pl.pallas_call(
        functools.partial(finish_kernel, groups, taps),
        in_specs=[pl.BlockSpec(own.shape, lambda: (0, 0))] * 2
        + [pl.BlockSpec(memory_space=pl.ANY)],
        out_specs=[
            pl.BlockSpec((groups, lanes), lambda: (0, 0)),
            pl.BlockSpec((taps, groups), lambda: (0, 0)),
            pl.BlockSpec(memory_space=pl.ANY),
        ],
        out_shape=[
            jax.ShapeDtypeStruct((groups, lanes), own.dtype),
            jax.ShapeDtypeStruct((taps, groups), own.dtype),
            jax.ShapeDtypeStruct(held.shape, held.dtype),
        ],
        input_output_aliases={2: 2},
        compiler_params=pltpu.CompilerParams(vmem_limit_bytes=16 << 20),
        cost_estimate=SMALL,
        name="finish_sums",
    )(own, other, held)


def permuted(block, pairs):
    return lax.ppermute(block, "ctx", pairs)


def local(inputs, upstream, medium_filter, short_filter):
    rows, width = inputs.shape
    groups, med = medium_filter.shape
    taps = short_filter.shape[1]
    devices = lax.axis_size("ctx")
    assert rows == med and med % 128 == 0 and groups <= med
    assert taps <= 8 and width % LANES == 0
    steps = 4 if width % (4 * LANES) == 0 else 1
    cols = width // steps
    tile = cols // GROUP
    lanes = med + 128
    factor = float(GROUP * rows * devices) ** -0.5
    forward = [(i, i + 1) for i in range(devices - 1)]
    backward = [(i + 1, i) for i in range(devices - 1)]

    def params(mebibytes=40):
        return pltpu.CompilerParams(vmem_limit_bytes=mebibytes << 20)

    def block(extent, base=0):
        return pl.BlockSpec((extent, cols), lambda i: (0, base + i))

    def filters(extent, base=0):
        return pl.BlockSpec((tile, extent), lambda i: (base + i, 0))

    def tables(extent, base=0):
        return pl.BlockSpec((tile * ROWS, extent), lambda i: (base + i, 0))

    short_rows = jnp.pad(short_filter.T, ((0, 8 - taps), (0, 0)))
    previous = permuted(inputs, forward)
    pieces = [(0, 2), (2, 1), (3, 1)] if steps == 4 else [(0, 1)]
    *sends, turned, conv, medium, table, wide = pl.pallas_call(
        functools.partial(own_kernel, taps, pieces),
        grid=(steps,),
        in_specs=[
            filters(med),
            pl.BlockSpec((8, groups), lambda i: (0, 0)),
            block(rows),
            block(rows),
        ],
        out_specs=[
            pl.BlockSpec(
                (rows + ROWS, cols),
                lambda i, start=start, count=count: (0, jnp.clip(i - start, 0, count - 1)),
            )
            for start, count in pieces
        ]
        + [
            block(rows),
            block(rows),
            filters(med),
            tables(lanes),
            block(8),
        ],
        out_shape=[
            jax.ShapeDtypeStruct((rows + ROWS, count * cols), BF16) for _, count in pieces
        ]
        + [
            jax.ShapeDtypeStruct((rows, width), BF16),
            jax.ShapeDtypeStruct((rows, width), F32),
            jax.ShapeDtypeStruct((groups, med), F32),
            jax.ShapeDtypeStruct((groups * ROWS, lanes), BF16),
            jax.ShapeDtypeStruct((8, width), F32),
        ],
        scratch_shapes=[pltpu.VMEM((rows + ROWS, cols), BF16)],
        compiler_params=params(),
        cost_estimate=SMALL,
        name="own_block",
    )(medium_filter, short_rows, inputs, upstream)
    following = [permuted(sends[0], backward)]

    halo_in = [table, wide, previous, inputs, upstream, turned, conv, medium]
    halo_specs = [
        tables(med),
        block(8),
        block(med),
        block(rows),
        block(rows),
        block(rows),
        block(rows),
        filters(med),
    ]
    halo_out = [
        jax.ShapeDtypeStruct((rows + ROWS, width), BF16),
        jax.ShapeDtypeStruct((groups + 8, med), F32),
    ]
    halo_out_specs = [block(rows + ROWS), pl.BlockSpec((groups + 8, med), lambda i: (0, 0))]
    held = sends[1:2]
    gate_cot, sums, *held = pl.pallas_call(
        functools.partial(halo_kernel, taps, factor),
        grid=(steps,),
        in_specs=halo_specs + [pl.BlockSpec(memory_space=pl.ANY)] * len(held),
        out_specs=halo_out_specs + [pl.BlockSpec(memory_space=pl.ANY)] * len(held),
        out_shape=halo_out + [jax.ShapeDtypeStruct(h.shape, h.dtype) for h in held],
        input_output_aliases={8: 2} if held else {},
        compiler_params=params(),
        cost_estimate=SMALL,
        name="halo_sums",
    )(*halo_in, *held)
    sends[1:2] = held

    both = jnp.pad(medium_filter, ((0, 0), (0, lanes - med))) + jnp.pad(
        short_filter, ((0, 0), (med + ROWS, lanes - med - ROWS - taps))
    )

    def input_grad(which, gradient):
        first, count = pieces[which]
        in_specs = [
            filters(lanes, first),
            tables(lanes, first),
            block(8, first),
            block(rows, first),
            block(rows + ROWS, first),
            block(rows + ROWS),
            block(rows + ROWS),
        ]
        operands = [both, table, wide, inputs, gate_cot, sends[which], following[which]]
        if gradient is not None:
            in_specs.append(pl.BlockSpec(memory_space=pl.ANY))
            operands.append(gradient)
        return pl.pallas_call(
            functools.partial(back_kernel, taps),
            grid=(count,),
            in_specs=in_specs,
            out_specs=block(rows, first),
            out_shape=jax.ShapeDtypeStruct((rows, width), BF16),
            input_output_aliases={} if gradient is None else {7: 0},
            compiler_params=params(),
            cost_estimate=SMALL,
            name="input_grad",
        )(*operands)

    gradient, made = None, 0
    if devices & (devices - 1):
        stages = 1
        sums = lax.psum(sums, "ctx")
    else:
        stages = max(1, (devices - 1).bit_length())
    others = jnp.zeros_like(sums)
    for stage in range(stages):
        if devices & (devices - 1) == 0:
            others = permuted(sums, [(i, i ^ (1 << stage)) for i in range(devices)])
        if stage + 1 < len(pieces):
            following.append(permuted(sends[stage + 1], backward))
        last = stage == stages - 1
        while made < len(following) and (last or stage == stages - 2 and made == 0):
            gradient = input_grad(made, gradient)
            made += 1
        if last:
            break
        if stage + 2 < len(pieces):
            sums, sends[stage + 2] = add_after(sums, others, sends[stage + 2])
        elif gradient is None:
            sums = sums + others
        else:
            sums, gradient = add_after(sums, others, gradient)
    for piece in range(made, len(pieces)):
        if piece == len(following):
            following.append(permuted(sends[piece], backward))
        gradient = input_grad(piece, gradient)
    medium, short, gradient = finish(sums, others, gradient, groups, taps)
    return gradient, medium, short.T


def solution(mesh):
    return jax.shard_map(
        local,
        mesh=mesh,
        in_specs=(P("ctx", "fsdp"), P("ctx", "fsdp"), P("fsdp", None), P("fsdp", None)),
        out_specs=(P("ctx", "fsdp"), P("fsdp", None), P("fsdp", None)),
        check_vma=False,
    )
```

```python
import functools

import jax
import jax.numpy as jnp
from jax import lax
from jax.experimental import pallas as pl
from jax.experimental.pallas import tpu as pltpu
from jax.sharding import PartitionSpec as P

GROUP = 16
ROWS = 16
EDGE = 8
LANES = 128
PIECES = (8, 5, 3)
ISSUE = (0, 1, 2)
EARLY = 1
F32 = jnp.float32
BF16 = jnp.bfloat16
LONG = pl.CostEstimate(flops=1, bytes_accessed=16 << 20, transcendentals=0)
SMALL = pl.CostEstimate(flops=1, bytes_accessed=1, transcendentals=0)


def iota(shape, dim):
    return lax.broadcasted_iota(jnp.int32, shape, dim)


def split3(values):
    high = values.astype(BF16)
    rest = values - high.astype(F32)
    middle = rest.astype(BF16)
    low = (rest - middle.astype(F32)).astype(BF16)
    return jnp.concatenate([high, middle, low], axis=0)


def exact_dot(values, table):
    rows = values.shape[0]
    out = jnp.dot(split3(values), table, preferred_element_type=F32)
    return out[:rows] + out[rows : 2 * rows] + out[2 * rows :]


def delayed(values, distance):
    return values if distance == 0 else pltpu.roll(values, distance, 0)


def toeplitz(base):
    lanes = base.shape[1]
    blocks = [
        pltpu.roll(
            jnp.broadcast_to(base[g : g + 1], (ROWS, lanes)), 0, 1, stride=1, stride_axis=0
        )
        for g in range(base.shape[0])
    ]
    return jnp.concatenate(blocks, 0).astype(BF16)


def own_group(product, lane_group):
    total = product[:ROWS]
    for g in range(1, product.shape[0] // ROWS):
        total = jnp.where(lane_group == g, product[g * ROWS : (g + 1) * ROWS], total)
    return total


def stacked(first, second, start, stop):
    extent = first.shape[0]
    if stop <= extent:
        return first[start:stop]
    if start >= extent:
        return second[start - extent : stop - extent]
    return jnp.concatenate([first[start:], second[: stop - extent]], 0)


def masked(cots, lane_group):
    return jnp.concatenate(
        [
            jnp.where(lane_group == g, cots, jnp.zeros_like(cots))
            for g in range(LANES // GROUP)
        ],
        0,
    )


def contracted(alone, part):
    return lax.dot_general(
        alone, part, (((1,), (1,)), ((), ())), preferred_element_type=F32
    )


def diagonal_sums(pairs, lanes):
    if pairs.shape[1] < lanes:
        pad = jnp.zeros((pairs.shape[0], lanes - pairs.shape[1]), F32)
        pairs = jnp.concatenate([pairs, pad], 1)
    return [
        jnp.sum(
            pltpu.roll(pairs[g * ROWS : (g + 1) * ROWS], 0, 1, stride=1, stride_axis=0),
            0,
            keepdims=True,
        )
        for g in range(LANES // GROUP)
    ]


def medium_sums(diagonals, med, lanes):
    flip_back = iota((lanes, med), 0) == med + ROWS - 1 - iota((lanes, med), 1)
    return exact_dot(jnp.concatenate(diagonals, 0), flip_back.astype(BF16))


def turning(extent):
    return (iota((extent, extent), 0) ^ (ROWS - 1) == iota((extent, extent), 1)).astype(BF16)


def gated(wide, near, taps):
    gate = wide[0:1] * near[ROWS:]
    for j in range(1, taps):
        gate = gate + wide[j : j + 1] * delayed(near, j)[ROWS:]
    return gate


def lane_groups():
    return iota((ROWS, 2 * LANES), 1) % LANES // GROUP


def own_kernel(taps, pieces, strip, ms_ref, st_ref, x_ref, u_ref, *outs):
    *send_refs, cot_ref, turned_ref, conv_ref, medium_ref, table_ref, back_ref, wide_ref = outs
    rows, width = x_ref.shape
    groups, med = medium_ref.shape
    window = med + ROWS
    lanes = med + 128
    tile = LANES // GROUP

    flip = (iota((med, lanes), 0) == med - iota((med, lanes), 1)).astype(BF16)
    spread = iota((groups, width), 0) == iota((groups, width), 1) // GROUP
    wide_ref[...] = jnp.dot(st_ref[...], spread.astype(BF16), preferred_element_type=F32)
    upturn = turning(rows)
    lane_group = lane_groups()

    def one_strip(step, carry):
        mine = pl.ds(pl.multiple_of(step * (strip // GROUP), tile), strip // GROUP)
        back = ms_ref[mine, :]
        base = jnp.dot(back[:, :med], flip, preferred_element_type=F32)
        back = back.astype(F32)
        diagonals = []
        for block in range(strip // LANES):
            at = pl.ds(pl.multiple_of(step * strip + block * LANES, LANES), LANES)
            x = x_ref[:, at]
            near = jnp.concatenate([jnp.zeros((ROWS, LANES), F32), x.astype(F32)], 0)
            cot = u_ref[:, at].astype(F32) * gated(wide_ref[:, at], near, taps)
            cot = cot.astype(BF16)
            cot_ref[:, at] = cot
            turned = jnp.dot(upturn, cot, preferred_element_type=F32).astype(BF16)
            turned_ref[:, at] = turned
            table = toeplitz(base[block * tile : (block + 1) * tile])
            table_ref[at, :] = table
            back_ref[at, :] = toeplitz(back[block * tile : (block + 1) * tile])

            pairs = jnp.zeros((LANES, window), F32)
            for a in range(0, rows // ROWS, 2):
                lo, mid, hi = (ROWS * k for k in (a, a + 1, a + 2))
                empty = jnp.zeros((med - lo, LANES), BF16)
                part = jnp.concatenate(
                    [
                        jnp.concatenate([empty, x[:mid]], 0),
                        jnp.concatenate([empty, x[ROWS:hi]], 0),
                    ],
                    1,
                )
                conv = own_group(
                    jnp.dot(table[:, :window], part, preferred_element_type=F32), lane_group
                )
                conv_ref[lo:mid, at] = conv[:, :LANES]
                conv_ref[mid:hi, at] = conv[:, LANES:]
                if a:
                    both = jnp.concatenate([turned[lo:mid], turned[mid:hi]], 1)
                    pairs = pairs + contracted(masked(both, lane_group), part)
            diagonals += diagonal_sums(pairs, lanes)
        medium_ref[mine, :] = medium_sums(diagonals, med, lanes)
        return carry

    lax.fori_loop(0, width // strip, one_strip, 0)
    for send_ref, (start, stop) in zip(send_refs, pieces):
        for at in range(start, stop, LANES):
            block = slice(at, at + LANES)
            parts = [cot_ref[:, block], x_ref[:ROWS, block], u_ref[:ROWS, block]]
            cot, x, u = (part.astype(F32) for part in parts)
            send_ref[:, at - start : at - start + LANES] = jnp.concatenate(
                [cot[EDGE:], x[:EDGE], u[:EDGE]], 0
            ).astype(BF16)


def halo_kernel(taps, factor, cols, table_ref, wide_ref, prev_ref, x_ref, u_ref, turned_ref,
                conv_ref, medium_ref, *rest):
    gate_cot_ref, sums_ref = rest[len(rest) // 2 - 1 :][:2]
    rows, width = x_ref.shape
    med = prev_ref.shape[0]
    window = med + ROWS
    lanes = med + 128
    tile = LANES // GROUP
    groups = cols // GROUP
    total_groups = sums_ref.shape[0] - 8
    upturn = turning(ROWS)
    lane_group = lane_groups()

    def one_step(step, total):
        diagonals, short = [], []
        for block in range(cols // LANES):
            start = step * cols + block * LANES
            at = slice(start, start + LANES)
            prev, x, u = prev_ref[:, at], x_ref[:, at], u_ref[:, at]
            near = jnp.concatenate([prev[med - ROWS :], x], 0).astype(F32)
            table = table_ref[at, :med]
            head = gated(wide_ref[:, at], near[: 2 * ROWS], taps) * u[:ROWS].astype(F32)
            head = head.astype(BF16)
            gate_cot_ref[:ROWS, at] = head
            head = jnp.dot(upturn, head, preferred_element_type=F32).astype(BF16)

            pairs = None
            gate_cots = []
            for a in range(0, rows // ROWS, 2):
                lo, mid, hi = (ROWS * k for k in (a, a + 1, a + 2))
                part = jnp.concatenate(
                    [stacked(prev, x, lo, med), stacked(prev, x, mid, med + ROWS)], 1
                )
                conv = own_group(
                    jnp.dot(table[:, : med - lo], part, preferred_element_type=F32),
                    lane_group,
                )
                if a == 0:
                    part = jnp.concatenate([part, jnp.concatenate([x[:ROWS], x[ROWS:hi]], 1)], 0)
                    both = jnp.concatenate([head, turned_ref[mid:hi, at]], 1)
                else:
                    both = jnp.concatenate([turned_ref[lo:mid, at], turned_ref[mid:hi, at]], 1)
                more = contracted(masked(both, lane_group), part)
                if more.shape[1] < window:
                    more = jnp.concatenate(
                        [more, jnp.zeros((LANES, window - more.shape[1]), F32)], 1
                    )
                pairs = more if pairs is None else pairs + more
                for k in range(2):
                    here = slice(lo + k * ROWS, mid + k * ROWS)
                    whole = conv_ref[here, at] + conv[:, k * LANES : (k + 1) * LANES]
                    gate_cots.append((u[here].astype(F32) * whole).astype(BF16))
            gate_cot = jnp.concatenate(gate_cots, 0)
            gate_cot_ref[ROWS:, at] = gate_cot
            diagonals += diagonal_sums(pairs, lanes)
            gate_cot = gate_cot.astype(F32)
            sums = [
                jnp.sum(gate_cot * delayed(near, j)[ROWS:], 0, keepdims=True)
                for j in range(taps)
            ]
            short.append(jnp.concatenate(sums + [jnp.zeros((8 - taps, LANES), F32)], 0))

        mine = slice(step * groups, (step + 1) * groups)
        medium = medium_ref[mine, :] + medium_sums(diagonals, med, lanes)
        sums_ref[mine, :] = medium * factor
        gather = iota((cols, med), 1) == step * groups + iota((cols, med), 0) // GROUP
        return total + exact_dot(jnp.concatenate(short, 1), gather.astype(BF16))

    total = jnp.zeros((8, med), F32)
    for step in range(width // cols):
        total = one_step(step, total)
    sums_ref[total_groups:, :] = total * factor


def back_kernel(taps, pieces, table_ref, back_ref, wide_ref, x_ref, gate_cot_ref, cot_ref, *rest):
    count = len(pieces)
    next_refs = rest[:count]
    out_ref, made, sems = rest[-3:]
    rows = x_ref.shape[0]
    window = table_ref.shape[1] - 128 + ROWS
    lane_group = lane_groups()
    first = pieces[0][0]
    blocks = [
        (start, next_ref, at)
        for (start, stop), next_ref in zip(pieces, next_refs)
        for at in range(start, stop, LANES)
    ]
    rest_of = jnp.zeros((ROWS - EDGE, LANES), F32)
    copies = []
    for index, (start, next_ref, begin) in enumerate(blocks):
        at = slice(begin, begin + LANES)
        there = slice(begin - first, begin - first + LANES)
        forward = table_ref[at, :window]
        table = back_ref[at, : window + 2 * ROWS]
        x = x_ref[:, at]
        later = next_ref[:, begin - start : begin - start + LANES].astype(F32)
        x_next, u_next = later[rows - EDGE : rows], later[rows:]
        near = jnp.concatenate([x[rows - ROWS :].astype(F32), x_next], 0)
        head = (u_next * gated(wide_ref[:, at], near, taps)).astype(BF16)
        part = jnp.concatenate(
            [x[rows + ROWS - window :], jnp.concatenate([x_next, rest_of], 0).astype(BF16)], 0
        )
        conv = own_group(
            jnp.dot(forward, part, preferred_element_type=F32), lane_group[:, :LANES]
        )
        gate_after = jnp.concatenate([u_next * conv[:EDGE], rest_of], 0).astype(BF16)
        cot = jnp.concatenate([gate_cot_ref[:ROWS, at], cot_ref[ROWS:, at]], 0)
        after = jnp.concatenate([head.astype(F32), later[: rows - EDGE]], 0).astype(BF16)
        gate_cot = gate_cot_ref[ROWS:, at]
        for a in range(0, rows // ROWS, 2):
            sides = [
                jnp.concatenate(
                    [
                        stacked(cot, after, k, k + window),
                        stacked(gate_cot, gate_after, k, k + 2 * ROWS),
                    ],
                    0,
                )
                for k in (a * ROWS, (a + 1) * ROWS)
            ]
            product = jnp.dot(
                table, jnp.concatenate(sides, 1), preferred_element_type=F32
            )
            out = own_group(product, lane_group).astype(BF16)
            made[a * ROWS : (a + 1) * ROWS, there] = out[:, :LANES]
            made[(a + 1) * ROWS : (a + 2) * ROWS, there] = out[:, LANES:]
        if index % 2 or index == len(blocks) - 1:
            since = blocks[index - index % 2][2]
            copy = pltpu.make_async_copy(
                made.at[:, since - first : begin + LANES - first],
                out_ref.at[:, since : begin + LANES],
                sems.at[index // 2],
            )
            copy.start()
            copies.append(copy)
    for copy in copies:
        copy.wait()


def add_kernel(own_ref, other_ref, *rest):
    out_ref = rest[len(rest) // 2]
    out_ref[...] = own_ref[...] + other_ref[...]


def add_after(own, other, *held):
    whole = pl.BlockSpec(own.shape, lambda: (0, 0))
    anywhere = [pl.BlockSpec(memory_space=pl.ANY)] * len(held)
    return pl.pallas_call(
        add_kernel,
        in_specs=[whole] * 2 + anywhere,
        out_specs=[whole] + anywhere,
        out_shape=[jax.ShapeDtypeStruct(a.shape, a.dtype) for a in (own, *held)],
        input_output_aliases={2 + k: 1 + k for k in range(len(held))},
        compiler_params=pltpu.CompilerParams(vmem_limit_bytes=16 << 20),
        cost_estimate=LONG,
        name="add_sums",
    )(own, other, *held)


def finish_kernel(groups, taps, own_ref, other_ref, held_ref, medium_ref, short_ref, held_out_ref):
    total = own_ref[...] + other_ref[...]
    medium_ref[...] = total[:groups]
    short_ref[...] = total[groups : groups + taps, :groups]


def finish(own, other, held, groups, taps):
    lanes = own.shape[1]
    return pl.pallas_call(
        functools.partial(finish_kernel, groups, taps),
        in_specs=[pl.BlockSpec(own.shape, lambda: (0, 0))] * 2
        + [pl.BlockSpec(memory_space=pl.ANY)],
        out_specs=[
            pl.BlockSpec((groups, lanes), lambda: (0, 0)),
            pl.BlockSpec((taps, groups), lambda: (0, 0)),
            pl.BlockSpec(memory_space=pl.ANY),
        ],
        out_shape=[
            jax.ShapeDtypeStruct((groups, lanes), own.dtype),
            jax.ShapeDtypeStruct((taps, groups), own.dtype),
            jax.ShapeDtypeStruct(held.shape, held.dtype),
        ],
        input_output_aliases={2: 2},
        compiler_params=pltpu.CompilerParams(vmem_limit_bytes=16 << 20),
        cost_estimate=LONG,
        name="finish_sums",
    )(own, other, held)


def permuted(block, pairs):
    return lax.ppermute(block, "ctx", pairs)


def local(inputs, upstream, medium_filter, short_filter):
    rows, width = inputs.shape
    groups, med = medium_filter.shape
    taps = short_filter.shape[1]
    devices = lax.axis_size("ctx")
    assert rows == med and med % 128 == 0 and groups <= med
    assert taps <= 8 and width % LANES == 0
    strip = min(width, 8 * LANES)
    lanes = med + 128
    factor = float(GROUP * rows * devices) ** -0.5
    forward = [(i, i + 1) for i in range(devices - 1)]
    backward = [(i + 1, i) for i in range(devices - 1)]

    def params(mebibytes=40):
        return pltpu.CompilerParams(vmem_limit_bytes=mebibytes << 20)

    short_rows = jnp.pad(short_filter.T, ((0, 8 - taps), (0, 0)))
    previous = permuted(inputs, forward)
    resident = pl.BlockSpec(memory_space=pltpu.VMEM)
    sizes = PIECES if width == LANES * sum(PIECES) else (width // LANES,)
    ends = [LANES * sum(sizes[: k + 1]) for k in range(len(sizes))]
    pieces = [(end - LANES * size, end) for end, size in zip(ends, sizes)]
    both = jnp.pad(medium_filter, ((0, 0), (0, lanes - med))) + jnp.pad(
        short_filter, ((0, 0), (med + ROWS, lanes - med - ROWS - taps))
    )
    *sends, cot, turned, conv, medium, table, back, wide = pl.pallas_call(
        functools.partial(own_kernel, taps, pieces, min(width, 4 * LANES)),
        in_specs=[resident] * 4,
        out_specs=[resident] * (len(pieces) + 7),
        out_shape=[
            jax.ShapeDtypeStruct((rows + EDGE, stop - start), BF16) for start, stop in pieces
        ]
        + [
            jax.ShapeDtypeStruct((rows, width), BF16),
            jax.ShapeDtypeStruct((rows, width), BF16),
            jax.ShapeDtypeStruct((rows, width), F32),
            jax.ShapeDtypeStruct((groups, med), F32),
            jax.ShapeDtypeStruct((groups * ROWS, lanes), BF16),
            jax.ShapeDtypeStruct((groups * ROWS, lanes), BF16),
            jax.ShapeDtypeStruct((8, width), F32),
        ],
        compiler_params=params(),
        cost_estimate=SMALL,
        name="own_block",
    )(both, short_rows, inputs, upstream)
    following = [permuted(sends[0], backward)]

    halo_in = [table, wide, previous, inputs, upstream, turned, conv, medium]
    waiting = [k for k in range(len(pieces)) if ISSUE[k] == 1]
    held = [sends[k] for k in waiting]
    gate_cot, sums, *held = pl.pallas_call(
        functools.partial(halo_kernel, taps, factor, strip),
        in_specs=[resident] * len(halo_in) + [pl.BlockSpec(memory_space=pl.ANY)] * len(held),
        out_specs=[resident] * 2 + [pl.BlockSpec(memory_space=pl.ANY)] * len(held),
        out_shape=[
            jax.ShapeDtypeStruct((rows + ROWS, width), BF16),
            jax.ShapeDtypeStruct((groups + 8, med), F32),
        ]
        + [jax.ShapeDtypeStruct(h.shape, h.dtype) for h in held],
        input_output_aliases={8 + k: 2 + k for k in range(len(held))},
        compiler_params=params(),
        cost_estimate=SMALL,
        name="halo_sums",
    )(*halo_in, *held)
    for k, value in zip(waiting, held):
        sends[k] = value

    def input_grad(which, gradient):
        mine = [pieces[k] for k in which]
        extent = mine[-1][1] - mine[0][0]
        operands = [table, back, wide, inputs, gate_cot, cot]
        operands += [following[k] for k in which]
        in_specs = [resident] * len(operands)
        aliases = {}
        if gradient is not None:
            aliases[len(operands)] = 0
            in_specs.append(pl.BlockSpec(memory_space=pl.ANY))
            operands.append(gradient)
        return pl.pallas_call(
            functools.partial(back_kernel, taps, mine),
            in_specs=in_specs,
            out_specs=pl.BlockSpec(memory_space=pl.ANY),
            out_shape=jax.ShapeDtypeStruct((rows, width), BF16),
            input_output_aliases=aliases,
            scratch_shapes=[
                pltpu.VMEM((rows, extent), BF16),
                pltpu.SemaphoreType.DMA((-(-extent // (2 * LANES)),)),
            ],
            compiler_params=params(),
            cost_estimate=SMALL,
            name="input_grad",
        )(*operands)

    gradient = None
    if devices & (devices - 1):
        stages = 1
        sums = lax.psum(sums, "ctx")
    else:
        stages = max(1, (devices - 1).bit_length())
    others = jnp.zeros_like(sums)
    for stage in range(stages):
        if devices & (devices - 1) == 0:
            others = permuted(sums, [(i, i ^ (1 << ((0, 1, 2)[stage] if stages == 3 else stage))) for i in range(devices)])
        if len(following) < len(pieces) and ISSUE[len(following)] == stage + 1:
            following.append(permuted(sends[len(following)], backward))
        last = stage == stages - 1
        if len(pieces) > 1 and stage == EARLY and not last:
            gradient = input_grad([0], None)
        if last:
            break
        waiting = [k for k in range(len(pieces)) if ISSUE[k] == stage + 2]
        held = [sends[k] for k in waiting] + ([] if gradient is None else [gradient])
        sums, *held = add_after(sums, others, *held)
        if gradient is not None:
            gradient = held.pop()
        for k, value in zip(waiting, held):
            sends[k] = value
    for k in range(len(following), len(pieces)):
        following.append(permuted(sends[k], backward))
    rest = range(len(pieces)) if gradient is None else range(1, len(pieces))
    gradient = input_grad(list(rest), gradient)
    medium, short, gradient = finish(sums, others, gradient, groups, taps)
    return gradient, medium, short.T


def solution(mesh):
    return jax.shard_map(
        local,
        mesh=mesh,
        in_specs=(P("ctx", "fsdp"), P("ctx", "fsdp"), P("fsdp", None), P("fsdp", None)),
        out_specs=(P("ctx", "fsdp"), P("fsdp", None), P("fsdp", None)),
        check_vma=False,
    )
```

```python
import functools

import jax
import jax.numpy as jnp
from jax import lax
from jax.experimental import pallas as pl
from jax.experimental.pallas import tpu as pltpu
from jax.sharding import PartitionSpec as P

GROUP = 16
ROWS = 16
EDGE = 8
LANES = 128
F32 = jnp.float32
BF16 = jnp.bfloat16
LONG = pl.CostEstimate(flops=1, bytes_accessed=16 << 20, transcendentals=0)
SMALL = pl.CostEstimate(flops=1, bytes_accessed=1, transcendentals=0)


def iota(shape, dim):
    return lax.broadcasted_iota(jnp.int32, shape, dim)


def split3(values):
    high = values.astype(BF16)
    rest = values - high.astype(F32)
    middle = rest.astype(BF16)
    low = (rest - middle.astype(F32)).astype(BF16)
    return jnp.concatenate([high, middle, low], axis=0)


def exact_dot(values, table):
    rows = values.shape[0]
    out = jnp.dot(split3(values), table, preferred_element_type=F32)
    return out[:rows] + out[rows : 2 * rows] + out[2 * rows :]


def delayed(values, distance):
    return values if distance == 0 else pltpu.roll(values, distance, 0)


def toeplitz(base):
    lanes = base.shape[1]
    blocks = [
        pltpu.roll(
            jnp.broadcast_to(base[g : g + 1], (ROWS, lanes)), 0, 1, stride=1, stride_axis=0
        )
        for g in range(base.shape[0])
    ]
    return jnp.concatenate(blocks, 0).astype(BF16)


def own_group(product, lane_group):
    total = product[:ROWS]
    for g in range(1, product.shape[0] // ROWS):
        total = jnp.where(lane_group == g, product[g * ROWS : (g + 1) * ROWS], total)
    return total


def stacked(first, second, start, stop):
    extent = first.shape[0]
    if stop <= extent:
        return first[start:stop]
    if start >= extent:
        return second[start - extent : stop - extent]
    return jnp.concatenate([first[start:], second[: stop - extent]], 0)


def masked(cots, lane_group):
    return jnp.concatenate(
        [
            jnp.where(lane_group == g, cots, jnp.zeros_like(cots))
            for g in range(LANES // GROUP)
        ],
        0,
    )


def contracted(alone, part):
    return lax.dot_general(
        alone, part, (((1,), (1,)), ((), ())), preferred_element_type=F32
    )


def diagonal_sums(pairs, lanes):
    if pairs.shape[1] < lanes:
        pad = jnp.zeros((pairs.shape[0], lanes - pairs.shape[1]), F32)
        pairs = jnp.concatenate([pairs, pad], 1)
    return [
        jnp.sum(
            pltpu.roll(pairs[g * ROWS : (g + 1) * ROWS], 0, 1, stride=1, stride_axis=0),
            0,
            keepdims=True,
        )
        for g in range(LANES // GROUP)
    ]


def medium_sums(diagonals, med, lanes):
    flip_back = iota((lanes, med), 0) == med + ROWS - 1 - iota((lanes, med), 1)
    return exact_dot(jnp.concatenate(diagonals, 0), flip_back.astype(BF16))


def turning(extent):
    return (iota((extent, extent), 0) ^ (ROWS - 1) == iota((extent, extent), 1)).astype(BF16)


def gated(wide, near, taps):
    gate = wide[0:1] * near[ROWS:]
    for j in range(1, taps):
        gate = gate + wide[j : j + 1] * delayed(near, j)[ROWS:]
    return gate


def lane_groups():
    return iota((ROWS, 2 * LANES), 1) % LANES // GROUP


def own_kernel(taps, pieces, strip, ms_ref, st_ref, x_ref, u_ref, *outs):
    *send_refs, cot_ref, turned_ref, conv_ref, medium_ref, table_ref, back_ref, wide_ref = outs
    rows, width = x_ref.shape
    groups, med = medium_ref.shape
    window = med + ROWS
    lanes = med + 128
    tile = LANES // GROUP

    flip = (iota((med, lanes), 0) == med - iota((med, lanes), 1)).astype(BF16)
    spread = iota((groups, width), 0) == iota((groups, width), 1) // GROUP
    wide_ref[...] = jnp.dot(st_ref[...], spread.astype(BF16), preferred_element_type=F32)
    upturn = turning(rows)
    lane_group = lane_groups()

    def one_strip(step, carry):
        mine = pl.ds(pl.multiple_of(step * (strip // GROUP), tile), strip // GROUP)
        back = ms_ref[mine, :]
        base = jnp.dot(back[:, :med], flip, preferred_element_type=F32)
        back = back.astype(F32)
        diagonals = []
        for block in range(strip // LANES):
            at = pl.ds(pl.multiple_of(step * strip + block * LANES, LANES), LANES)
            x = x_ref[:, at]
            near = jnp.concatenate([jnp.zeros((ROWS, LANES), F32), x.astype(F32)], 0)
            cot = u_ref[:, at].astype(F32) * gated(wide_ref[:, at], near, taps)
            cot = cot.astype(BF16)
            cot_ref[:, at] = cot
            turned = jnp.dot(upturn, cot, preferred_element_type=F32).astype(BF16)
            turned_ref[:, at] = turned
            table = toeplitz(base[block * tile : (block + 1) * tile])
            table_ref[at, :] = table
            back_ref[at, :] = toeplitz(back[block * tile : (block + 1) * tile])

            pairs = jnp.zeros((LANES, window), F32)
            for a in range(0, rows // ROWS, 2):
                lo, mid, hi = (ROWS * k for k in (a, a + 1, a + 2))
                empty = jnp.zeros((med - lo, LANES), BF16)
                part = jnp.concatenate(
                    [
                        jnp.concatenate([empty, x[:mid]], 0),
                        jnp.concatenate([empty, x[ROWS:hi]], 0),
                    ],
                    1,
                )
                conv = own_group(
                    jnp.dot(table[:, :window], part, preferred_element_type=F32), lane_group
                )
                conv_ref[lo:mid, at] = conv[:, :LANES]
                conv_ref[mid:hi, at] = conv[:, LANES:]
                if a:
                    both = jnp.concatenate([turned[lo:mid], turned[mid:hi]], 1)
                    pairs = pairs + contracted(masked(both, lane_group), part)
            diagonals += diagonal_sums(pairs, lanes)
        medium_ref[mine, :] = medium_sums(diagonals, med, lanes)
        return carry

    lax.fori_loop(0, width // strip, one_strip, 0)
    for send_ref, (start, stop) in zip(send_refs, pieces):
        for at in range(start, stop, LANES):
            block = slice(at, at + LANES)
            parts = [cot_ref[:, block], x_ref[:ROWS, block], u_ref[:ROWS, block]]
            cot, x, u = (part.astype(F32) for part in parts)
            send_ref[:, at - start : at - start + LANES] = jnp.concatenate(
                [cot[EDGE:], x[:EDGE], u[:EDGE]], 0
            ).astype(BF16)


def halo_kernel(taps, factor, table_ref, wide_ref, prev_ref, x_ref, u_ref, turned_ref,
                conv_ref, medium_ref, *rest):
    gate_cot_ref, sums_ref = rest[len(rest) // 2 - 1 :][:2]
    rows, width = x_ref.shape
    med = prev_ref.shape[0]
    window = med + ROWS
    lanes = med + 128
    total_groups = sums_ref.shape[0] - 8
    upturn = turning(ROWS)
    lane_group = lane_groups()

    diagonals, short = [], []
    for start in range(0, width, LANES):
        at = slice(start, start + LANES)
        prev, x, u = prev_ref[:, at], x_ref[:, at], u_ref[:, at]
        near = jnp.concatenate([prev[med - ROWS :], x], 0).astype(F32)
        table = table_ref[at, :med]
        head = gated(wide_ref[:, at], near[: 2 * ROWS], taps) * u[:ROWS].astype(F32)
        head = head.astype(BF16)
        gate_cot_ref[:ROWS, at] = head
        head = jnp.dot(upturn, head, preferred_element_type=F32).astype(BF16)

        pairs = None
        gate_cots = []
        for a in range(0, rows // ROWS, 2):
            lo, mid, hi = (ROWS * k for k in (a, a + 1, a + 2))
            part = jnp.concatenate(
                [stacked(prev, x, lo, med), stacked(prev, x, mid, med + ROWS)], 1
            )
            conv = own_group(
                jnp.dot(table[:, : med - lo], part, preferred_element_type=F32),
                lane_group,
            )
            if a == 0:
                part = jnp.concatenate([part, jnp.concatenate([x[:ROWS], x[ROWS:hi]], 1)], 0)
                both = jnp.concatenate([head, turned_ref[mid:hi, at]], 1)
            else:
                both = jnp.concatenate([turned_ref[lo:mid, at], turned_ref[mid:hi, at]], 1)
            more = contracted(masked(both, lane_group), part)
            if more.shape[1] < window:
                more = jnp.concatenate(
                    [more, jnp.zeros((LANES, window - more.shape[1]), F32)], 1
                )
            pairs = more if pairs is None else pairs + more
            for k in range(2):
                here = slice(lo + k * ROWS, mid + k * ROWS)
                whole = conv_ref[here, at] + conv[:, k * LANES : (k + 1) * LANES]
                gate_cots.append((u[here].astype(F32) * whole).astype(BF16))
        gate_cot = jnp.concatenate(gate_cots, 0)
        gate_cot_ref[ROWS:, at] = gate_cot
        diagonals += diagonal_sums(pairs, lanes)
        gate_cot = gate_cot.astype(F32)
        sums = [
            jnp.sum(gate_cot * delayed(near, j)[ROWS:], 0, keepdims=True)
            for j in range(taps)
        ]
        short.append(jnp.concatenate(sums + [jnp.zeros((8 - taps, LANES), F32)], 0))

    sums_ref[:total_groups, :] = (medium_ref[...] + medium_sums(diagonals, med, lanes)) * factor
    gather = (iota((LANES, med), 1) == iota((LANES, med), 0) // GROUP).astype(BF16)
    gathered = exact_dot(jnp.concatenate(short, 0), gather)
    total = gathered[:8]
    for block in range(1, width // LANES):
        part = gathered[8 * block : 8 * (block + 1)]
        total = total + pltpu.roll(part, block * (LANES // GROUP), 1)
    sums_ref[total_groups:, :] = total * factor


def back_kernel(taps, pieces, table_ref, back_ref, wide_ref, x_ref, gate_cot_ref, cot_ref, *rest):
    count = len(pieces)
    next_refs = rest[:count]
    out_ref, made, sems = rest[-3:]
    rows = x_ref.shape[0]
    window = table_ref.shape[1] - 128 + ROWS
    lane_group = lane_groups()
    first = pieces[0][0]
    blocks = [
        (start, next_ref, at)
        for (start, stop), next_ref in zip(pieces, next_refs)
        for at in range(start, stop, LANES)
    ]
    rest_of = jnp.zeros((ROWS - EDGE, LANES), F32)
    copies = []
    for index, (start, next_ref, begin) in enumerate(blocks):
        at = slice(begin, begin + LANES)
        there = slice(begin - first, begin - first + LANES)
        forward = table_ref[at, :window]
        table = back_ref[at, : window + 2 * ROWS]
        x = x_ref[:, at]
        later = next_ref[:, begin - start : begin - start + LANES].astype(F32)
        x_next, u_next = later[rows - EDGE : rows], later[rows:]
        near = jnp.concatenate([x[rows - ROWS :].astype(F32), x_next], 0)
        head = (u_next * gated(wide_ref[:, at], near, taps)).astype(BF16)
        part = jnp.concatenate(
            [x[rows + ROWS - window :], jnp.concatenate([x_next, rest_of], 0).astype(BF16)], 0
        )
        conv = own_group(
            jnp.dot(forward, part, preferred_element_type=F32), lane_group[:, :LANES]
        )
        gate_after = jnp.concatenate([u_next * conv[:EDGE], rest_of], 0).astype(BF16)
        cot = jnp.concatenate([gate_cot_ref[:ROWS, at], cot_ref[ROWS:, at]], 0)
        after = jnp.concatenate([head.astype(F32), later[: rows - EDGE]], 0).astype(BF16)
        gate_cot = gate_cot_ref[ROWS:, at]
        for a in range(0, rows // ROWS, 2):
            sides = [
                jnp.concatenate(
                    [
                        stacked(cot, after, k, k + window),
                        stacked(gate_cot, gate_after, k, k + 2 * ROWS),
                    ],
                    0,
                )
                for k in (a * ROWS, (a + 1) * ROWS)
            ]
            product = jnp.dot(
                table, jnp.concatenate(sides, 1), preferred_element_type=F32
            )
            out = own_group(product, lane_group).astype(BF16)
            made[a * ROWS : (a + 1) * ROWS, there] = out[:, :LANES]
            made[(a + 1) * ROWS : (a + 2) * ROWS, there] = out[:, LANES:]
        if index % 2 or index == len(blocks) - 1:
            since = blocks[index - index % 2][2]
            copy = pltpu.make_async_copy(
                made.at[:, since - first : begin + LANES - first],
                out_ref.at[:, since : begin + LANES],
                sems.at[index // 2],
            )
            copy.start()
            copies.append(copy)
    for copy in copies:
        copy.wait()


def add_kernel(own_ref, other_ref, *rest):
    out_ref = rest[len(rest) // 2]
    out_ref[...] = own_ref[...] + other_ref[...]


def add_after(own, other, *held):
    whole = pl.BlockSpec(own.shape, lambda: (0, 0))
    anywhere = [pl.BlockSpec(memory_space=pl.ANY)] * len(held)
    return pl.pallas_call(
        add_kernel,
        in_specs=[whole] * 2 + anywhere,
        out_specs=[whole] + anywhere,
        out_shape=[jax.ShapeDtypeStruct(a.shape, a.dtype) for a in (own, *held)],
        input_output_aliases={2 + k: 1 + k for k in range(len(held))},
        compiler_params=pltpu.CompilerParams(vmem_limit_bytes=16 << 20),
        cost_estimate=LONG,
        name="add_sums",
    )(own, other, *held)


def finish_kernel(groups, taps, own_ref, other_ref, held_ref, medium_ref, short_ref, held_out_ref):
    total = own_ref[...] + other_ref[...]
    medium_ref[...] = total[:groups]
    short_ref[...] = total[groups : groups + taps, :groups]


def finish(own, other, held, groups, taps):
    lanes = own.shape[1]
    return pl.pallas_call(
        functools.partial(finish_kernel, groups, taps),
        in_specs=[pl.BlockSpec(own.shape, lambda: (0, 0))] * 2
        + [pl.BlockSpec(memory_space=pl.ANY)],
        out_specs=[
            pl.BlockSpec((groups, lanes), lambda: (0, 0)),
            pl.BlockSpec((taps, groups), lambda: (0, 0)),
            pl.BlockSpec(memory_space=pl.ANY),
        ],
        out_shape=[
            jax.ShapeDtypeStruct((groups, lanes), own.dtype),
            jax.ShapeDtypeStruct((taps, groups), own.dtype),
            jax.ShapeDtypeStruct(held.shape, held.dtype),
        ],
        input_output_aliases={2: 2},
        compiler_params=pltpu.CompilerParams(vmem_limit_bytes=16 << 20),
        cost_estimate=LONG,
        name="finish_sums",
    )(own, other, held)


def permuted(block, pairs):
    return lax.ppermute(block, "ctx", pairs)


def local(inputs, upstream, medium_filter, short_filter):
    rows, width = inputs.shape
    groups, med = medium_filter.shape
    taps = short_filter.shape[1]
    devices = lax.axis_size("ctx")
    assert rows == med and med % 128 == 0 and groups <= med
    assert taps <= 8 and width % LANES == 0
    lanes = med + 128
    factor = float(GROUP * rows * devices) ** -0.5
    forward = [(i, i + 1) for i in range(devices - 1)]
    backward = [(i + 1, i) for i in range(devices - 1)]

    def params():
        return pltpu.CompilerParams(vmem_limit_bytes=40 << 20)

    short_rows = jnp.pad(short_filter.T, ((0, 8 - taps), (0, 0)))
    previous = permuted(inputs, forward)
    resident = pl.BlockSpec(memory_space=pltpu.VMEM)
    count = width // LANES
    sizes = (count // 2, 5 * count // 16, 3 * count // 16) if count % 16 == 0 else (count,)
    ends = [LANES * sum(sizes[: k + 1]) for k in range(len(sizes))]
    pieces = [(end - LANES * size, end) for end, size in zip(ends, sizes)]
    both = jnp.pad(medium_filter, ((0, 0), (0, lanes - med))) + jnp.pad(
        short_filter, ((0, 0), (med + ROWS, lanes - med - ROWS - taps))
    )
    *sends, cot, turned, conv, medium, table, back, wide = pl.pallas_call(
        functools.partial(own_kernel, taps, pieces, min(width, 4 * LANES)),
        in_specs=[resident] * 4,
        out_specs=[resident] * (len(pieces) + 7),
        out_shape=[
            jax.ShapeDtypeStruct((rows + EDGE, stop - start), BF16) for start, stop in pieces
        ]
        + [
            jax.ShapeDtypeStruct((rows, width), BF16),
            jax.ShapeDtypeStruct((rows, width), BF16),
            jax.ShapeDtypeStruct((rows, width), F32),
            jax.ShapeDtypeStruct((groups, med), F32),
            jax.ShapeDtypeStruct((groups * ROWS, lanes), BF16),
            jax.ShapeDtypeStruct((groups * ROWS, lanes), BF16),
            jax.ShapeDtypeStruct((8, width), F32),
        ],
        compiler_params=params(),
        cost_estimate=SMALL,
        name="own_block",
    )(both, short_rows, inputs, upstream)
    following = [permuted(sends[0], backward)]

    halo_in = [table, wide, previous, inputs, upstream, turned, conv, medium]
    waiting = [k for k in range(len(pieces)) if k == 1]
    held = [sends[k] for k in waiting]
    gate_cot, sums, *held = pl.pallas_call(
        functools.partial(halo_kernel, taps, factor),
        in_specs=[resident] * len(halo_in) + [pl.BlockSpec(memory_space=pl.ANY)] * len(held),
        out_specs=[resident] * 2 + [pl.BlockSpec(memory_space=pl.ANY)] * len(held),
        out_shape=[
            jax.ShapeDtypeStruct((rows + ROWS, width), BF16),
            jax.ShapeDtypeStruct((groups + 8, med), F32),
        ]
        + [jax.ShapeDtypeStruct(h.shape, h.dtype) for h in held],
        input_output_aliases={8 + k: 2 + k for k in range(len(held))},
        compiler_params=params(),
        cost_estimate=SMALL,
        name="halo_sums",
    )(*halo_in, *held)
    for k, value in zip(waiting, held):
        sends[k] = value

    def input_grad(which, gradient):
        mine = [pieces[k] for k in which]
        extent = mine[-1][1] - mine[0][0]
        operands = [table, back, wide, inputs, gate_cot, cot]
        operands += [following[k] for k in which]
        in_specs = [resident] * len(operands)
        aliases = {}
        if gradient is not None:
            aliases[len(operands)] = 0
            in_specs.append(pl.BlockSpec(memory_space=pl.ANY))
            operands.append(gradient)
        return pl.pallas_call(
            functools.partial(back_kernel, taps, mine),
            in_specs=in_specs,
            out_specs=pl.BlockSpec(memory_space=pl.ANY),
            out_shape=jax.ShapeDtypeStruct((rows, width), BF16),
            input_output_aliases=aliases,
            scratch_shapes=[
                pltpu.VMEM((rows, extent), BF16),
                pltpu.SemaphoreType.DMA((-(-extent // (2 * LANES)),)),
            ],
            compiler_params=params(),
            cost_estimate=SMALL,
            name="input_grad",
        )(*operands)

    gradient = None
    if devices & (devices - 1):
        stages = 1
        sums = lax.psum(sums, "ctx")
    else:
        stages = max(1, (devices - 1).bit_length())
    others = jnp.zeros_like(sums)
    for stage in range(stages):
        if devices & (devices - 1) == 0:
            others = permuted(sums, [(i, i ^ (1 << stage)) for i in range(devices)])
        if stage + 1 < len(pieces):
            following.append(permuted(sends[stage + 1], backward))
        last = stage == stages - 1
        if len(pieces) > 1 and stage == 1 and not last:
            gradient = input_grad([0], None)
        if last:
            break
        waiting = [k for k in range(len(pieces)) if k == stage + 2]
        held = [sends[k] for k in waiting] + ([] if gradient is None else [gradient])
        sums, *held = add_after(sums, others, *held)
        if gradient is not None:
            gradient = held.pop()
        for k, value in zip(waiting, held):
            sends[k] = value
    for k in range(len(following), len(pieces)):
        following.append(permuted(sends[k], backward))
    rest = range(len(pieces)) if gradient is None else range(1, len(pieces))
    gradient = input_grad(list(rest), gradient)
    medium, short, gradient = finish(sums, others, gradient, groups, taps)
    return gradient, medium, short.T


def solution(mesh):
    return jax.shard_map(
        local,
        mesh=mesh,
        in_specs=(P("ctx", "fsdp"), P("ctx", "fsdp"), P("fsdp", None), P("fsdp", None)),
        out_specs=(P("ctx", "fsdp"), P("fsdp", None), P("fsdp", None)),
        check_vma=False,
    )
```

```python
import functools

import jax
import jax.numpy as jnp
from jax import lax
from jax.experimental import pallas as pl
from jax.experimental.pallas import tpu as pltpu
from jax.sharding import PartitionSpec as P

GROUP = 16
ROWS = 16
EDGE = 8
LANES = 128
F32 = jnp.float32
BF16 = jnp.bfloat16
LONG = pl.CostEstimate(flops=1, bytes_accessed=16 << 20, transcendentals=0)
SMALL = pl.CostEstimate(flops=1, bytes_accessed=1, transcendentals=0)


def iota(shape, dim):
    return lax.broadcasted_iota(jnp.int32, shape, dim)


def split3(values):
    high = values.astype(BF16)
    rest = values - high.astype(F32)
    middle = rest.astype(BF16)
    low = (rest - middle.astype(F32)).astype(BF16)
    return jnp.concatenate([high, middle, low], axis=0)


def exact_dot(values, table):
    rows = values.shape[0]
    out = jnp.dot(split3(values), table, preferred_element_type=F32)
    return out[:rows] + out[rows : 2 * rows] + out[2 * rows :]


def delayed(values, distance):
    return values if distance == 0 else pltpu.roll(values, distance, 0)


def toeplitz(base):
    lanes = base.shape[1]
    blocks = [
        pltpu.roll(
            jnp.broadcast_to(base[g : g + 1], (ROWS, lanes)), 0, 1, stride=1, stride_axis=0
        )
        for g in range(base.shape[0])
    ]
    return jnp.concatenate(blocks, 0).astype(BF16)


def own_group(product, lane_group):
    total = product[:ROWS]
    for g in range(1, product.shape[0] // ROWS):
        total = jnp.where(lane_group == g, product[g * ROWS : (g + 1) * ROWS], total)
    return total


def stacked(first, second, start, stop):
    extent = first.shape[0]
    if stop <= extent:
        return first[start:stop]
    if start >= extent:
        return second[start - extent : stop - extent]
    return jnp.concatenate([first[start:], second[: stop - extent]], 0)


def masked(cots, lane_group):
    return jnp.concatenate(
        [
            jnp.where(lane_group == g, cots, jnp.zeros_like(cots))
            for g in range(LANES // GROUP)
        ],
        0,
    )


def contracted(alone, part):
    return lax.dot_general(
        alone, part, (((1,), (1,)), ((), ())), preferred_element_type=F32
    )


def diagonal_sums(pairs, lanes):
    if pairs.shape[1] < lanes:
        pad = jnp.zeros((pairs.shape[0], lanes - pairs.shape[1]), F32)
        pairs = jnp.concatenate([pairs, pad], 1)
    return [
        jnp.sum(
            pltpu.roll(pairs[g * ROWS : (g + 1) * ROWS], 0, 1, stride=1, stride_axis=0),
            0,
            keepdims=True,
        )
        for g in range(LANES // GROUP)
    ]


def medium_sums(diagonals, med, lanes):
    flip_back = iota((lanes, med), 0) == med + ROWS - 1 - iota((lanes, med), 1)
    return exact_dot(jnp.concatenate(diagonals, 0), flip_back.astype(BF16))


def turning(extent):
    return (iota((extent, extent), 0) ^ (ROWS - 1) == iota((extent, extent), 1)).astype(BF16)


def gated(wide, near, taps):
    gate = wide[0:1] * near[ROWS:]
    for j in range(1, taps):
        gate = gate + wide[j : j + 1] * delayed(near, j)[ROWS:]
    return gate


def lane_groups():
    return iota((ROWS, 2 * LANES), 1) % LANES // GROUP


def own_kernel(taps, pieces, strip, ms_ref, st_ref, x_ref, u_ref, *outs):
    *send_refs, cot_ref, turned_ref, conv_ref, medium_ref, table_ref, back_ref, wide_ref = outs
    rows, width = x_ref.shape
    groups, med = medium_ref.shape
    window = med + ROWS
    lanes = med + 128
    tile = LANES // GROUP

    flip = (iota((med, lanes), 0) == med - iota((med, lanes), 1)).astype(BF16)
    spread = iota((groups, width), 0) == iota((groups, width), 1) // GROUP
    wide_ref[...] = jnp.dot(st_ref[...], spread.astype(BF16), preferred_element_type=F32)
    upturn = turning(rows)
    lane_group = lane_groups()

    def one_strip(step, carry):
        mine = pl.ds(pl.multiple_of(step * (strip // GROUP), tile), strip // GROUP)
        back = ms_ref[mine, :]
        base = jnp.dot(back[:, :med], flip, preferred_element_type=F32)
        back = back.astype(F32)
        diagonals = []
        for block in range(strip // LANES):
            at = pl.ds(pl.multiple_of(step * strip + block * LANES, LANES), LANES)
            x = x_ref[:, at]
            near = jnp.concatenate([jnp.zeros((ROWS, LANES), F32), x.astype(F32)], 0)
            cot = u_ref[:, at].astype(F32) * gated(wide_ref[:, at], near, taps)
            cot = cot.astype(BF16)
            cot_ref[:, at] = cot
            turned = jnp.dot(upturn, cot, preferred_element_type=F32).astype(BF16)
            turned_ref[:, at] = turned
            table = toeplitz(base[block * tile : (block + 1) * tile])
            table_ref[at, :] = table
            back_ref[at, :] = toeplitz(back[block * tile : (block + 1) * tile])

            pairs = jnp.zeros((LANES, window), F32)
            for a in range(0, rows // ROWS, 2):
                lo, mid, hi = (ROWS * k for k in (a, a + 1, a + 2))
                empty = jnp.zeros((med - lo, LANES), BF16)
                part = jnp.concatenate(
                    [
                        jnp.concatenate([empty, x[:mid]], 0),
                        jnp.concatenate([empty, x[ROWS:hi]], 0),
                    ],
                    1,
                )
                conv = own_group(
                    jnp.dot(table[:, :window], part, preferred_element_type=F32), lane_group
                )
                conv_ref[lo:mid, at] = conv[:, :LANES]
                conv_ref[mid:hi, at] = conv[:, LANES:]
                if a:
                    both = jnp.concatenate([turned[lo:mid], turned[mid:hi]], 1)
                    pairs = pairs + contracted(masked(both, lane_group), part)
            diagonals += diagonal_sums(pairs, lanes)
        medium_ref[mine, :] = medium_sums(diagonals, med, lanes)
        return carry

    lax.fori_loop(0, width // strip, one_strip, 0)
    for send_ref, (start, stop) in zip(send_refs, pieces):
        for at in range(start, stop, LANES):
            block = slice(at, at + LANES)
            parts = [cot_ref[:, block], x_ref[:ROWS, block], u_ref[:ROWS, block]]
            cot, x, u = (part.astype(F32) for part in parts)
            send_ref[:, at - start : at - start + LANES] = jnp.concatenate(
                [cot[EDGE:], x[:EDGE], u[:EDGE]], 0
            ).astype(BF16)


def halo_kernel(taps, factor, table_ref, wide_ref, prev_ref, x_ref, u_ref, turned_ref,
                conv_ref, medium_ref, *rest):
    gate_cot_ref, sums_ref = rest[len(rest) // 2 - 1 :][:2]
    rows, width = x_ref.shape
    med = prev_ref.shape[0]
    window = med + ROWS
    lanes = med + 128
    total_groups = sums_ref.shape[0] - 8
    upturn = turning(ROWS)
    lane_group = lane_groups()

    diagonals, short = [], []
    for start in range(0, width, LANES):
        at = slice(start, start + LANES)
        prev, x, u = prev_ref[:, at], x_ref[:, at], u_ref[:, at]
        near = jnp.concatenate([prev[med - ROWS :], x], 0).astype(F32)
        table = table_ref[at, :med]
        head = gated(wide_ref[:, at], near[: 2 * ROWS], taps) * u[:ROWS].astype(F32)
        head = head.astype(BF16)
        gate_cot_ref[:ROWS, at] = head
        head = jnp.dot(upturn, head, preferred_element_type=F32).astype(BF16)

        pairs = None
        gate_cots = []
        for a in range(0, rows // ROWS, 2):
            lo, mid, hi = (ROWS * k for k in (a, a + 1, a + 2))
            part = jnp.concatenate(
                [stacked(prev, x, lo, med), stacked(prev, x, mid, med + ROWS)], 1
            )
            conv = own_group(
                jnp.dot(table[:, : med - lo], part, preferred_element_type=F32),
                lane_group,
            )
            if a == 0:
                part = jnp.concatenate([part, jnp.concatenate([x[:ROWS], x[ROWS:hi]], 1)], 0)
                both = jnp.concatenate([head, turned_ref[mid:hi, at]], 1)
            else:
                both = jnp.concatenate([turned_ref[lo:mid, at], turned_ref[mid:hi, at]], 1)
            more = contracted(masked(both, lane_group), part)
            if more.shape[1] < window:
                more = jnp.concatenate(
                    [more, jnp.zeros((LANES, window - more.shape[1]), F32)], 1
                )
            pairs = more if pairs is None else pairs + more
            for k in range(2):
                here = slice(lo + k * ROWS, mid + k * ROWS)
                whole = conv_ref[here, at] + conv[:, k * LANES : (k + 1) * LANES]
                gate_cots.append((u[here].astype(F32) * whole).astype(BF16))
        gate_cot = jnp.concatenate(gate_cots, 0)
        gate_cot_ref[ROWS:, at] = gate_cot
        diagonals += diagonal_sums(pairs, lanes)
        gate_cot = gate_cot.astype(F32)
        sums = [
            jnp.sum(gate_cot * delayed(near, j)[ROWS:], 0, keepdims=True)
            for j in range(taps)
        ]
        short.append(jnp.concatenate(sums + [jnp.zeros((8 - taps, LANES), F32)], 0))

    sums_ref[:total_groups, :] = (medium_ref[...] + medium_sums(diagonals, med, lanes)) * factor
    gather = (iota((LANES, med), 1) == iota((LANES, med), 0) // GROUP).astype(BF16)
    gathered = exact_dot(jnp.concatenate(short, 0), gather)
    total = gathered[:8]
    for block in range(1, width // LANES):
        part = gathered[8 * block : 8 * (block + 1)]
        total = total + pltpu.roll(part, block * (LANES // GROUP), 1)
    sums_ref[total_groups:, :] = total * factor


def back_kernel(taps, pieces, table_ref, back_ref, wide_ref, x_ref, gate_cot_ref, cot_ref, *rest):
    count = len(pieces)
    next_refs = rest[:count]
    out_ref, made, sems = rest[-3:]
    rows = x_ref.shape[0]
    window = table_ref.shape[1] - 128 + ROWS
    lane_group = lane_groups()
    first = pieces[0][0]
    blocks = [
        (start, next_ref, at)
        for (start, stop), next_ref in zip(pieces, next_refs)
        for at in range(start, stop, LANES)
    ]
    rest_of = jnp.zeros((ROWS - EDGE, LANES), F32)
    copies = []
    for index, (start, next_ref, begin) in enumerate(blocks):
        at = slice(begin, begin + LANES)
        there = slice(begin - first, begin - first + LANES)
        forward = table_ref[at, :window]
        table = back_ref[at, : window + 2 * ROWS]
        x = x_ref[:, at]
        later = next_ref[:, begin - start : begin - start + LANES].astype(F32)
        x_next, u_next = later[rows - EDGE : rows], later[rows:]
        near = jnp.concatenate([x[rows - ROWS :].astype(F32), x_next], 0)
        head = (u_next * gated(wide_ref[:, at], near, taps)).astype(BF16)
        part = jnp.concatenate(
            [x[rows + ROWS - window :], jnp.concatenate([x_next, rest_of], 0).astype(BF16)], 0
        )
        conv = own_group(
            jnp.dot(forward, part, preferred_element_type=F32), lane_group[:, :LANES]
        )
        gate_after = jnp.concatenate([u_next * conv[:EDGE], rest_of], 0).astype(BF16)
        cot = jnp.concatenate([gate_cot_ref[:ROWS, at], cot_ref[ROWS:, at]], 0)
        after = jnp.concatenate([head.astype(F32), later[: rows - EDGE]], 0).astype(BF16)
        gate_cot = gate_cot_ref[ROWS:, at]
        for a in range(0, rows // ROWS, 2):
            sides = [
                jnp.concatenate(
                    [
                        stacked(cot, after, k, k + window),
                        stacked(gate_cot, gate_after, k, k + 2 * ROWS),
                    ],
                    0,
                )
                for k in (a * ROWS, (a + 1) * ROWS)
            ]
            product = jnp.dot(
                table, jnp.concatenate(sides, 1), preferred_element_type=F32
            )
            out = own_group(product, lane_group).astype(BF16)
            made[a * ROWS : (a + 1) * ROWS, there] = out[:, :LANES]
            made[(a + 1) * ROWS : (a + 2) * ROWS, there] = out[:, LANES:]
        if index % 2 or index == len(blocks) - 1:
            since = blocks[index - index % 2][2]
            copy = pltpu.make_async_copy(
                made.at[:, since - first : begin + LANES - first],
                out_ref.at[:, since : begin + LANES],
                sems.at[index // 2],
            )
            copy.start()
            copies.append(copy)
    for copy in copies:
        copy.wait()


def add_kernel(own_ref, other_ref, *rest):
    out_ref = rest[len(rest) // 2]
    out_ref[...] = own_ref[...] + other_ref[...]


def add_after(own, other, *held):
    whole = pl.BlockSpec(own.shape, lambda: (0, 0))
    anywhere = [pl.BlockSpec(memory_space=pl.ANY)] * len(held)
    return pl.pallas_call(
        add_kernel,
        in_specs=[whole] * 2 + anywhere,
        out_specs=[whole] + anywhere,
        out_shape=[jax.ShapeDtypeStruct(a.shape, a.dtype) for a in (own, *held)],
        input_output_aliases={2 + k: 1 + k for k in range(len(held))},
        compiler_params=pltpu.CompilerParams(vmem_limit_bytes=16 << 20),
        cost_estimate=LONG,
        name="add_sums",
    )(own, other, *held)


def finish_kernel(groups, taps, own_ref, other_ref, held_ref, medium_ref, short_ref, held_out_ref):
    total = own_ref[...] + other_ref[...]
    medium_ref[...] = total[:groups]
    short_ref[...] = total[groups : groups + taps, :groups]


def finish(own, other, held, groups, taps):
    lanes = own.shape[1]
    return pl.pallas_call(
        functools.partial(finish_kernel, groups, taps),
        in_specs=[pl.BlockSpec(own.shape, lambda: (0, 0))] * 2
        + [pl.BlockSpec(memory_space=pl.ANY)],
        out_specs=[
            pl.BlockSpec((groups, lanes), lambda: (0, 0)),
            pl.BlockSpec((taps, groups), lambda: (0, 0)),
            pl.BlockSpec(memory_space=pl.ANY),
        ],
        out_shape=[
            jax.ShapeDtypeStruct((groups, lanes), own.dtype),
            jax.ShapeDtypeStruct((taps, groups), own.dtype),
            jax.ShapeDtypeStruct(held.shape, held.dtype),
        ],
        input_output_aliases={2: 2},
        compiler_params=pltpu.CompilerParams(vmem_limit_bytes=16 << 20),
        cost_estimate=LONG,
        name="finish_sums",
    )(own, other, held)


def permuted(block, pairs):
    return lax.ppermute(block, "ctx", pairs)


def local(inputs, upstream, medium_filter, short_filter):
    rows, width = inputs.shape
    groups, med = medium_filter.shape
    taps = short_filter.shape[1]
    devices = lax.axis_size("ctx")
    assert rows == med and med % 128 == 0 and groups <= med
    assert taps <= 8 and width % LANES == 0
    lanes = med + 128
    factor = float(GROUP * rows * devices) ** -0.5
    forward = [(i, i + 1) for i in range(devices - 1)]
    backward = [(i + 1, i) for i in range(devices - 1)]

    def params():
        return pltpu.CompilerParams(vmem_limit_bytes=40 << 20)

    short_rows = jnp.pad(short_filter.T, ((0, 8 - taps), (0, 0)))
    previous = permuted(inputs, forward)
    resident = pl.BlockSpec(memory_space=pltpu.VMEM)
    count = width // LANES
    sizes = (count // 2, count // 4, count // 4) if count % 16 == 0 else (count,)
    ends = [LANES * sum(sizes[: k + 1]) for k in range(len(sizes))]
    pieces = [(end - LANES * size, end) for end, size in zip(ends, sizes)]
    both = jnp.pad(medium_filter, ((0, 0), (0, lanes - med))) + jnp.pad(
        short_filter, ((0, 0), (med + ROWS, lanes - med - ROWS - taps))
    )
    *sends, cot, turned, conv, medium, table, back, wide = pl.pallas_call(
        functools.partial(own_kernel, taps, pieces, min(width, 8 * LANES)),
        in_specs=[resident] * 4,
        out_specs=[resident] * (len(pieces) + 7),
        out_shape=[
            jax.ShapeDtypeStruct((rows + EDGE, stop - start), BF16) for start, stop in pieces
        ]
        + [
            jax.ShapeDtypeStruct((rows, width), BF16),
            jax.ShapeDtypeStruct((rows, width), BF16),
            jax.ShapeDtypeStruct((rows, width), F32),
            jax.ShapeDtypeStruct((groups, med), F32),
            jax.ShapeDtypeStruct((groups * ROWS, lanes), BF16),
            jax.ShapeDtypeStruct((groups * ROWS, lanes), BF16),
            jax.ShapeDtypeStruct((8, width), F32),
        ],
        compiler_params=params(),
        cost_estimate=SMALL,
        name="own_block",
    )(both, short_rows, inputs, upstream)
    following = [permuted(sends[0], backward)]

    halo_in = [table, wide, previous, inputs, upstream, turned, conv, medium]
    waiting = [k for k in range(len(pieces)) if k == 1]
    held = [sends[k] for k in waiting]
    gate_cot, sums, *held = pl.pallas_call(
        functools.partial(halo_kernel, taps, factor),
        in_specs=[resident] * len(halo_in) + [pl.BlockSpec(memory_space=pl.ANY)] * len(held),
        out_specs=[resident] * 2 + [pl.BlockSpec(memory_space=pl.ANY)] * len(held),
        out_shape=[
            jax.ShapeDtypeStruct((rows + ROWS, width), BF16),
            jax.ShapeDtypeStruct((groups + 8, med), F32),
        ]
        + [jax.ShapeDtypeStruct(h.shape, h.dtype) for h in held],
        input_output_aliases={8 + k: 2 + k for k in range(len(held))},
        compiler_params=params(),
        cost_estimate=SMALL,
        name="halo_sums",
    )(*halo_in, *held)
    for k, value in zip(waiting, held):
        sends[k] = value

    def input_grad(which, gradient):
        mine = [pieces[k] for k in which]
        extent = mine[-1][1] - mine[0][0]
        operands = [table, back, wide, inputs, gate_cot, cot]
        operands += [following[k] for k in which]
        in_specs = [resident] * len(operands)
        aliases = {}
        if gradient is not None:
            aliases[len(operands)] = 0
            in_specs.append(pl.BlockSpec(memory_space=pl.ANY))
            operands.append(gradient)
        return pl.pallas_call(
            functools.partial(back_kernel, taps, mine),
            in_specs=in_specs,
            out_specs=pl.BlockSpec(memory_space=pl.ANY),
            out_shape=jax.ShapeDtypeStruct((rows, width), BF16),
            input_output_aliases=aliases,
            scratch_shapes=[
                pltpu.VMEM((rows, extent), BF16),
                pltpu.SemaphoreType.DMA((-(-extent // (2 * LANES)),)),
            ],
            compiler_params=params(),
            cost_estimate=SMALL,
            name="input_grad",
        )(*operands)

    gradient = None
    if devices & (devices - 1):
        stages = 1
        sums = lax.psum(sums, "ctx")
    else:
        stages = max(1, (devices - 1).bit_length())
    others = jnp.zeros_like(sums)
    for stage in range(stages):
        if devices & (devices - 1) == 0:
            others = permuted(sums, [(i, i ^ (1 << stage)) for i in range(devices)])
        if stage + 1 < len(pieces):
            following.append(permuted(sends[stage + 1], backward))
        last = stage == stages - 1
        if len(pieces) > 1 and stage == 1 and not last:
            gradient = input_grad([0], None)
        if last:
            break
        waiting = [k for k in range(len(pieces)) if k == stage + 2]
        held = [sends[k] for k in waiting] + ([] if gradient is None else [gradient])
        sums, *held = add_after(sums, others, *held)
        if gradient is not None:
            gradient = held.pop()
        for k, value in zip(waiting, held):
            sends[k] = value
    for k in range(len(following), len(pieces)):
        following.append(permuted(sends[k], backward))
    rest = range(len(pieces)) if gradient is None else range(1, len(pieces))
    gradient = input_grad(list(rest), gradient)
    medium, short, gradient = finish(sums, others, gradient, groups, taps)
    return gradient, medium, short.T


def solution(mesh):
    return jax.shard_map(
        local,
        mesh=mesh,
        in_specs=(P("ctx", "fsdp"), P("ctx", "fsdp"), P("fsdp", None), P("fsdp", None)),
        out_specs=(P("ctx", "fsdp"), P("fsdp", None), P("fsdp", None)),
        check_vma=False,
    )
```

```python
import functools

import jax
import jax.numpy as jnp
from jax import lax
from jax.experimental import pallas as pl
from jax.experimental.pallas import tpu as pltpu
from jax.sharding import PartitionSpec as P

GROUP = 16
ROWS = 16
EDGE = 8
LANES = 128
F32 = jnp.float32
BF16 = jnp.bfloat16
LONG = pl.CostEstimate(flops=1, bytes_accessed=16 << 20, transcendentals=0)
SMALL = pl.CostEstimate(flops=1, bytes_accessed=1, transcendentals=0)


def iota(shape, dim):
    return lax.broadcasted_iota(jnp.int32, shape, dim)


def split3(values):
    high = values.astype(BF16)
    rest = values - high.astype(F32)
    middle = rest.astype(BF16)
    low = (rest - middle.astype(F32)).astype(BF16)
    return jnp.concatenate([high, middle, low], axis=0)


def exact_dot(values, table):
    rows = values.shape[0]
    out = jnp.dot(split3(values), table, preferred_element_type=F32)
    return out[:rows] + out[rows : 2 * rows] + out[2 * rows :]


def delayed(values, distance):
    return values if distance == 0 else pltpu.roll(values, distance, 0)


def toeplitz(base):
    lanes = base.shape[1]
    blocks = [
        pltpu.roll(
            jnp.broadcast_to(base[g : g + 1], (ROWS, lanes)), 0, 1, stride=1, stride_axis=0
        )
        for g in range(base.shape[0])
    ]
    return jnp.concatenate(blocks, 0).astype(BF16)


def own_group(product, lane_group):
    total = product[:ROWS]
    for g in range(1, product.shape[0] // ROWS):
        total = jnp.where(lane_group == g, product[g * ROWS : (g + 1) * ROWS], total)
    return total


def stacked(first, second, start, stop):
    extent = first.shape[0]
    if stop <= extent:
        return first[start:stop]
    if start >= extent:
        return second[start - extent : stop - extent]
    return jnp.concatenate([first[start:], second[: stop - extent]], 0)


def masked(cots, lane_group):
    return jnp.concatenate(
        [
            jnp.where(lane_group == g, cots, jnp.zeros_like(cots))
            for g in range(LANES // GROUP)
        ],
        0,
    )


def contracted(alone, part):
    return lax.dot_general(
        alone, part, (((1,), (1,)), ((), ())), preferred_element_type=F32
    )


def diagonal_sums(pairs, lanes):
    if pairs.shape[1] < lanes:
        pad = jnp.zeros((pairs.shape[0], lanes - pairs.shape[1]), F32)
        pairs = jnp.concatenate([pairs, pad], 1)
    return [
        jnp.sum(
            pltpu.roll(pairs[g * ROWS : (g + 1) * ROWS], 0, 1, stride=1, stride_axis=0),
            0,
            keepdims=True,
        )
        for g in range(LANES // GROUP)
    ]


def medium_sums(diagonals, med, lanes):
    flip_back = iota((lanes, med), 0) == med + ROWS - 1 - iota((lanes, med), 1)
    return exact_dot(jnp.concatenate(diagonals, 0), flip_back.astype(BF16))


def turning(extent):
    return (iota((extent, extent), 0) ^ (ROWS - 1) == iota((extent, extent), 1)).astype(BF16)


def gated(wide, near, taps):
    gate = wide[0:1] * near[ROWS:]
    for j in range(1, taps):
        gate = gate + wide[j : j + 1] * delayed(near, j)[ROWS:]
    return gate


def lane_groups():
    return iota((ROWS, 2 * LANES), 1) % LANES // GROUP


def own_kernel(taps, pieces, strip, ms_ref, st_ref, x_ref, u_ref, *outs):
    *send_refs, cot_ref, turned_ref, conv_ref, medium_ref, table_ref, back_ref, wide_ref = outs
    rows, width = x_ref.shape
    groups, med = medium_ref.shape
    window = med + ROWS
    lanes = med + 128
    tile = LANES // GROUP

    flip = (iota((med, lanes), 0) == med - iota((med, lanes), 1)).astype(BF16)
    spread = iota((groups, width), 0) == iota((groups, width), 1) // GROUP
    wide_ref[...] = jnp.dot(st_ref[...], spread.astype(BF16), preferred_element_type=F32)
    upturn = turning(rows)
    lane_group = lane_groups()

    def one_strip(step, carry):
        mine = pl.ds(pl.multiple_of(step * (strip // GROUP), tile), strip // GROUP)
        back = ms_ref[mine, :]
        base = jnp.dot(back[:, :med], flip, preferred_element_type=F32)
        back = back.astype(F32)
        diagonals = []
        for block in range(strip // LANES):
            at = pl.ds(pl.multiple_of(step * strip + block * LANES, LANES), LANES)
            x = x_ref[:, at]
            near = jnp.concatenate([jnp.zeros((ROWS, LANES), F32), x.astype(F32)], 0)
            cot = u_ref[:, at].astype(F32) * gated(wide_ref[:, at], near, taps)
            cot = cot.astype(BF16)
            cot_ref[:, at] = cot
            turned = jnp.dot(upturn, cot, preferred_element_type=F32).astype(BF16)
            turned_ref[:, at] = turned
            table = toeplitz(base[block * tile : (block + 1) * tile])
            table_ref[at, :] = table
            back_ref[at, :] = toeplitz(back[block * tile : (block + 1) * tile])

            pairs = jnp.zeros((LANES, window), F32)
            for a in range(0, rows // ROWS, 2):
                lo, mid, hi = (ROWS * k for k in (a, a + 1, a + 2))
                empty = jnp.zeros((med - lo, LANES), BF16)
                part = jnp.concatenate(
                    [
                        jnp.concatenate([empty, x[:mid]], 0),
                        jnp.concatenate([empty, x[ROWS:hi]], 0),
                    ],
                    1,
                )
                conv = own_group(
                    jnp.dot(table[:, :window], part, preferred_element_type=F32), lane_group
                )
                conv_ref[lo:mid, at] = conv[:, :LANES]
                conv_ref[mid:hi, at] = conv[:, LANES:]
                if a:
                    both = jnp.concatenate([turned[lo:mid], turned[mid:hi]], 1)
                    pairs = pairs + contracted(masked(both, lane_group), part)
            diagonals += diagonal_sums(pairs, lanes)
        medium_ref[mine, :] = medium_sums(diagonals, med, lanes)
        return carry

    lax.fori_loop(0, width // strip, one_strip, 0)
    for send_ref, (start, stop) in zip(send_refs, pieces):
        for at in range(start, stop, LANES):
            block = slice(at, at + LANES)
            parts = [cot_ref[:, block], x_ref[:ROWS, block], u_ref[:ROWS, block]]
            cot, x, u = (part.astype(F32) for part in parts)
            send_ref[:, at - start : at - start + LANES] = jnp.concatenate(
                [cot[EDGE:], x[:EDGE], u[:EDGE]], 0
            ).astype(BF16)


def halo_kernel(taps, factor, table_ref, wide_ref, prev_ref, x_ref, u_ref, turned_ref,
                conv_ref, medium_ref, *rest):
    gate_cot_ref, sums_ref = rest[len(rest) // 2 - 1 :][:2]
    rows, width = x_ref.shape
    med = prev_ref.shape[0]
    window = med + ROWS
    lanes = med + 128
    total_groups = sums_ref.shape[0] - 8
    upturn = turning(ROWS)
    lane_group = lane_groups()

    diagonals, short = [], []
    for start in range(0, width, LANES):
        at = slice(start, start + LANES)
        prev, x, u = prev_ref[:, at], x_ref[:, at], u_ref[:, at]
        near = jnp.concatenate([prev[med - ROWS :], x], 0).astype(F32)
        table = table_ref[at, :med]
        head = gated(wide_ref[:, at], near[: 2 * ROWS], taps) * u[:ROWS].astype(F32)
        head = head.astype(BF16)
        gate_cot_ref[:ROWS, at] = head
        head = jnp.dot(upturn, head, preferred_element_type=F32).astype(BF16)

        pairs = None
        gate_cots = []
        for a in range(0, rows // ROWS, 2):
            lo, mid, hi = (ROWS * k for k in (a, a + 1, a + 2))
            part = jnp.concatenate(
                [stacked(prev, x, lo, med), stacked(prev, x, mid, med + ROWS)], 1
            )
            conv = own_group(
                jnp.dot(table[:, : med - lo], part, preferred_element_type=F32),
                lane_group,
            )
            if a == 0:
                part = jnp.concatenate([part, jnp.concatenate([x[:ROWS], x[ROWS:hi]], 1)], 0)
                both = jnp.concatenate([head, turned_ref[mid:hi, at]], 1)
            else:
                both = jnp.concatenate([turned_ref[lo:mid, at], turned_ref[mid:hi, at]], 1)
            more = contracted(masked(both, lane_group), part)
            if more.shape[1] < window:
                more = jnp.concatenate(
                    [more, jnp.zeros((LANES, window - more.shape[1]), F32)], 1
                )
            pairs = more if pairs is None else pairs + more
            for k in range(2):
                here = slice(lo + k * ROWS, mid + k * ROWS)
                whole = conv_ref[here, at] + conv[:, k * LANES : (k + 1) * LANES]
                gate_cots.append((u[here].astype(F32) * whole).astype(BF16))
        gate_cot = jnp.concatenate(gate_cots, 0)
        gate_cot_ref[ROWS:, at] = gate_cot
        diagonals += diagonal_sums(pairs, lanes)
        gate_cot = gate_cot.astype(F32)
        sums = [
            jnp.sum(gate_cot * delayed(near, j)[ROWS:], 0, keepdims=True)
            for j in range(taps)
        ]
        short.append(jnp.concatenate(sums + [jnp.zeros((8 - taps, LANES), F32)], 0))

    sums_ref[:total_groups, :] = (medium_ref[...] + medium_sums(diagonals, med, lanes)) * factor
    gather = (iota((LANES, med), 1) == iota((LANES, med), 0) // GROUP).astype(BF16)
    gathered = exact_dot(jnp.concatenate(short, 0), gather)
    total = gathered[:8]
    for block in range(1, width // LANES):
        part = gathered[8 * block : 8 * (block + 1)]
        total = total + pltpu.roll(part, block * (LANES // GROUP), 1)
    sums_ref[total_groups:, :] = total * factor


def back_kernel(taps, pieces, table_ref, back_ref, wide_ref, x_ref, gate_cot_ref, cot_ref, *rest):
    count = len(pieces)
    next_refs = rest[:count]
    out_ref, made, sems = rest[-3:]
    rows = x_ref.shape[0]
    window = table_ref.shape[1] - 128 + ROWS
    lane_group = lane_groups()
    first = pieces[0][0]
    blocks = [
        (start, next_ref, at)
        for (start, stop), next_ref in zip(pieces, next_refs)
        for at in range(start, stop, LANES)
    ]
    rest_of = jnp.zeros((ROWS - EDGE, LANES), F32)
    copies = []
    for index, (start, next_ref, begin) in enumerate(blocks):
        at = slice(begin, begin + LANES)
        there = slice(begin - first, begin - first + LANES)
        forward = table_ref[at, :window]
        table = back_ref[at, : window + 2 * ROWS]
        x = x_ref[:, at]
        later = next_ref[:, begin - start : begin - start + LANES].astype(F32)
        x_next, u_next = later[rows - EDGE : rows], later[rows:]
        near = jnp.concatenate([x[rows - ROWS :].astype(F32), x_next], 0)
        head = (u_next * gated(wide_ref[:, at], near, taps)).astype(BF16)
        part = jnp.concatenate(
            [x[rows + ROWS - window :], jnp.concatenate([x_next, rest_of], 0).astype(BF16)], 0
        )
        conv = own_group(
            jnp.dot(forward, part, preferred_element_type=F32), lane_group[:, :LANES]
        )
        gate_after = jnp.concatenate([u_next * conv[:EDGE], rest_of], 0).astype(BF16)
        cot = jnp.concatenate([gate_cot_ref[:ROWS, at], cot_ref[ROWS:, at]], 0)
        after = jnp.concatenate([head.astype(F32), later[: rows - EDGE]], 0).astype(BF16)
        gate_cot = gate_cot_ref[ROWS:, at]
        for a in range(0, rows // ROWS, 2):
            sides = [
                jnp.concatenate(
                    [
                        stacked(cot, after, k, k + window),
                        stacked(gate_cot, gate_after, k, k + 2 * ROWS),
                    ],
                    0,
                )
                for k in (a * ROWS, (a + 1) * ROWS)
            ]
            product = jnp.dot(
                table, jnp.concatenate(sides, 1), preferred_element_type=F32
            )
            out = own_group(product, lane_group).astype(BF16)
            made[a * ROWS : (a + 1) * ROWS, there] = out[:, :LANES]
            made[(a + 1) * ROWS : (a + 2) * ROWS, there] = out[:, LANES:]
        if index % 2 or index == len(blocks) - 1:
            since = blocks[index - index % 2][2]
            copy = pltpu.make_async_copy(
                made.at[:, since - first : begin + LANES - first],
                out_ref.at[:, since : begin + LANES],
                sems.at[index // 2],
            )
            copy.start()
            copies.append(copy)
    for copy in copies:
        copy.wait()


def add_kernel(own_ref, other_ref, *rest):
    out_ref = rest[len(rest) // 2]
    out_ref[...] = own_ref[...] + other_ref[...]


def add_after(own, other, *held):
    whole = pl.BlockSpec(own.shape, lambda: (0, 0))
    anywhere = [pl.BlockSpec(memory_space=pl.ANY)] * len(held)
    return pl.pallas_call(
        add_kernel,
        in_specs=[whole] * 2 + anywhere,
        out_specs=[whole] + anywhere,
        out_shape=[jax.ShapeDtypeStruct(a.shape, a.dtype) for a in (own, *held)],
        input_output_aliases={2 + k: 1 + k for k in range(len(held))},
        compiler_params=pltpu.CompilerParams(vmem_limit_bytes=16 << 20),
        cost_estimate=LONG,
        name="add_sums",
    )(own, other, *held)


def finish_kernel(groups, taps, own_ref, other_ref, held_ref, medium_ref, short_ref, held_out_ref):
    total = own_ref[...] + other_ref[...]
    medium_ref[...] = total[:groups]
    short_ref[...] = total[groups : groups + taps, :groups]


def finish(own, other, held, groups, taps):
    lanes = own.shape[1]
    return pl.pallas_call(
        functools.partial(finish_kernel, groups, taps),
        in_specs=[pl.BlockSpec(own.shape, lambda: (0, 0))] * 2
        + [pl.BlockSpec(memory_space=pl.ANY)],
        out_specs=[
            pl.BlockSpec((groups, lanes), lambda: (0, 0)),
            pl.BlockSpec((taps, groups), lambda: (0, 0)),
            pl.BlockSpec(memory_space=pl.ANY),
        ],
        out_shape=[
            jax.ShapeDtypeStruct((groups, lanes), own.dtype),
            jax.ShapeDtypeStruct((taps, groups), own.dtype),
            jax.ShapeDtypeStruct(held.shape, held.dtype),
        ],
        input_output_aliases={2: 2},
        compiler_params=pltpu.CompilerParams(vmem_limit_bytes=16 << 20),
        cost_estimate=LONG,
        name="finish_sums",
    )(own, other, held)


def permuted(block, pairs):
    return lax.ppermute(block, "ctx", pairs)


def local(inputs, upstream, medium_filter, short_filter):
    rows, width = inputs.shape
    groups, med = medium_filter.shape
    taps = short_filter.shape[1]
    devices = lax.axis_size("ctx")
    assert rows == med and med % 128 == 0 and groups <= med
    assert taps <= 8 and width % LANES == 0
    lanes = med + 128
    factor = float(GROUP * rows * devices) ** -0.5
    forward = [(i, i + 1) for i in range(devices - 1)]
    backward = [(i + 1, i) for i in range(devices - 1)]

    def params():
        return pltpu.CompilerParams(vmem_limit_bytes=40 << 20)

    short_rows = jnp.pad(short_filter.T, ((0, 8 - taps), (0, 0)))
    previous = permuted(inputs, forward)
    resident = pl.BlockSpec(memory_space=pltpu.VMEM)
    count = width // LANES
    sizes = (count // 2, count // 4, count // 4) if count % 16 == 0 else (count,)
    ends = [LANES * sum(sizes[: k + 1]) for k in range(len(sizes))]
    pieces = [(end - LANES * size, end) for end, size in zip(ends, sizes)]
    both = jnp.pad(medium_filter, ((0, 0), (0, lanes - med))) + jnp.pad(
        short_filter, ((0, 0), (med + ROWS, lanes - med - ROWS - taps))
    )
    *sends, cot, turned, conv, medium, table, back, wide = pl.pallas_call(
        functools.partial(own_kernel, taps, pieces, min(width, 8 * LANES)),
        in_specs=[resident] * 4,
        out_specs=[resident] * (len(pieces) + 7),
        out_shape=[
            jax.ShapeDtypeStruct((rows + EDGE, stop - start), BF16) for start, stop in pieces
        ]
        + [
            jax.ShapeDtypeStruct((rows, width), BF16),
            jax.ShapeDtypeStruct((rows, width), BF16),
            jax.ShapeDtypeStruct((rows, width), F32),
            jax.ShapeDtypeStruct((groups, med), F32),
            jax.ShapeDtypeStruct((groups * ROWS, lanes), BF16),
            jax.ShapeDtypeStruct((groups * ROWS, lanes), BF16),
            jax.ShapeDtypeStruct((8, width), F32),
        ],
        compiler_params=params(),
        cost_estimate=SMALL,
        name="own_block",
    )(both, short_rows, inputs, upstream)
    following = [permuted(sends[0], backward)]

    halo_in = [table, wide, previous, inputs, upstream, turned, conv, medium]
    waiting = [k for k in range(len(pieces)) if k == 1]
    held = [sends[k] for k in waiting]
    gate_cot, sums, *held = pl.pallas_call(
        functools.partial(halo_kernel, taps, factor),
        in_specs=[resident] * len(halo_in) + [pl.BlockSpec(memory_space=pl.ANY)] * len(held),
        out_specs=[resident] * 2 + [pl.BlockSpec(memory_space=pl.ANY)] * len(held),
        out_shape=[
            jax.ShapeDtypeStruct((rows + ROWS, width), BF16),
            jax.ShapeDtypeStruct((groups + 8, med), F32),
        ]
        + [jax.ShapeDtypeStruct(h.shape, h.dtype) for h in held],
        input_output_aliases={8 + k: 2 + k for k in range(len(held))},
        compiler_params=params(),
        cost_estimate=SMALL,
        name="halo_sums",
    )(*halo_in, *held)
    for k, value in zip(waiting, held):
        sends[k] = value

    def input_grad(which, gradient):
        mine = [pieces[k] for k in which]
        extent = mine[-1][1] - mine[0][0]
        operands = [table, back, wide, inputs, gate_cot, cot]
        operands += [following[k] for k in which]
        in_specs = [resident] * len(operands)
        aliases = {}
        if gradient is not None:
            aliases[len(operands)] = 0
            in_specs.append(pl.BlockSpec(memory_space=pl.ANY))
            operands.append(gradient)
        return pl.pallas_call(
            functools.partial(back_kernel, taps, mine),
            in_specs=in_specs,
            out_specs=pl.BlockSpec(memory_space=pl.ANY),
            out_shape=jax.ShapeDtypeStruct((rows, width), BF16),
            input_output_aliases=aliases,
            scratch_shapes=[
                pltpu.VMEM((rows, extent), BF16),
                pltpu.SemaphoreType.DMA((-(-extent // (2 * LANES)),)),
            ],
            compiler_params=params(),
            cost_estimate=SMALL,
            name="input_grad",
        )(*operands)

    gradient = None
    if devices & (devices - 1):
        stages = 1
        sums = lax.psum(sums, "ctx")
    else:
        stages = max(1, (devices - 1).bit_length())
    others = jnp.zeros_like(sums)
    for stage in range(stages):
        if devices & (devices - 1) == 0:
            others = permuted(sums, [(i, i ^ (1 << stage)) for i in range(devices)])
        if stage + 1 < len(pieces):
            following.append(permuted(sends[stage + 1], backward))
        last = stage == stages - 1
        if len(pieces) > 1 and stage == 0 and not last:
            gradient = input_grad([0], None)
        if last:
            break
        waiting = [k for k in range(len(pieces)) if k == stage + 2]
        held = [sends[k] for k in waiting] + ([] if gradient is None else [gradient])
        sums, *held = add_after(sums, others, *held)
        if gradient is not None:
            gradient = held.pop()
        for k, value in zip(waiting, held):
            sends[k] = value
    for k in range(len(following), len(pieces)):
        following.append(permuted(sends[k], backward))
    rest = range(len(pieces)) if gradient is None else range(1, len(pieces))
    gradient = input_grad(list(rest), gradient)
    medium, short, gradient = finish(sums, others, gradient, groups, taps)
    return gradient, medium, short.T


def solution(mesh):
    return jax.shard_map(
        local,
        mesh=mesh,
        in_specs=(P("ctx", "fsdp"), P("ctx", "fsdp"), P("fsdp", None), P("fsdp", None)),
        out_specs=(P("ctx", "fsdp"), P("fsdp", None), P("fsdp", None)),
        check_vma=False,
    )
```
